32 devices in a mesh: groups: 2 (over y), seq: 8 (over z, x), mp: 2 (over core).
Axes of the slice: x: 2, y: 2, z: 4, core: 2. Of those that a mesh axis runs over, the one named last changes fastest.
Arguments:
- queries: bfloat16 [32, 5120], P(('groups', 'seq'), 'mp'), parts along dimension 0, may hold values from -40 to 40
- prefix_keys: bfloat16 [4096, 1024], P(('groups', 'seq'), 'mp'), parts along dimension 0, may hold values from -10 to 10
- prefix_values: bfloat16 [4096, 1024], P(('groups', 'seq'), 'mp'), parts along dimension 0, may hold values from -6 to 6
- suffix_keys: bfloat16 [32, 8, 1024], P(('groups', 'seq'), None, 'mp'), parts along dimension 0, may hold values from -7 to 7
- suffix_values: bfloat16 [32, 8, 1024], P(('groups', 'seq'), None, 'mp'), parts along dimension 0, may hold values from -6 to 6
- new_keys: bfloat16 [32, 1024], P(('groups', 'seq'), 'mp'), parts along dimension 0, may hold values from -7 to 7
- new_values: bfloat16 [32, 1024], P(('groups', 'seq'), 'mp'), parts along dimension 0, may hold values from -6 to 6
- suffix_lengths: int32 [32], P(('groups', 'seq')), parts along dimension 0, may hold values from 0 to 7
- fork_list: int32 [16, 2], P(('groups', 'seq')), parts along dimension 0, may hold values from 0 to 15, as said below
Outputs:
- attended: bfloat16 [32, 5120], P(('groups', 'seq'), 'mp'), parts along dimension 0
- cache_keys: bfloat16 [32, 8, 1024], P(('groups', 'seq'), None, 'mp'), parts along dimension 0
- cache_values: bfloat16 [32, 8, 1024], P(('groups', 'seq'), None, 'mp'), parts along dimension 0
The draws below stay inside these ranges and needn't reach their ends.
There are 2 independent parts, one for each index of `groups`. The reference program is written for one: setup_inputs(seed, part) draws one part's arguments, and reference() takes and returns one part's arrays. A program takes and returns all parts, laid end to end along the dimension named above; each array names one. Nothing has to cross between parts.
Inputs may be any that keep to these rules, and one draw needn't show every extreme that they name: `fork_list`: row f has its parent among the branches f * 2 to f * 2 + 1; the children are distinct and none of them is a parent.
All inputs are finite; a program needn't handle non-finite values.
Results may differ from the reference program's by a relative error of at most 0.0044.
Values may be sent and summed in bfloat16 or wider, within the bound.
A program may use at most 64 MiB of HBM per device.

```python
import math
import jax
import jax.numpy as jnp
from jax import lax

HQ = 40
KVH = 8
HD = 128
PRE_DEV = 256
BR_DEV = 2
SUF = 8
PREFIX = 2048
BRANCHES = 16
FORKS = 8
N_SEQ = 8


def shared_directions(key):
    base = jax.random.fold_in(key, 101)
    suffix_dir = jnp.clip(jax.random.normal(jax.random.fold_in(base, 1), (KVH, HD), jnp.float32), -3.0, 3.0)
    return suffix_dir


def draw_queries(key, part):
    suffix_dir = shared_directions(key)
    noise = jnp.clip(jax.random.normal(jax.random.fold_in(key, 11), (BRANCHES, HQ, HD), jnp.float32), -4.0, 4.0)
    mixing = jax.random.uniform(jax.random.fold_in(key, 12), (BRANCHES, HQ, 1), jnp.float32, 0.0, 1.6)
    per_head = jnp.repeat(suffix_dir, HQ // KVH, axis=0)
    drawn = noise + mixing * per_head[None, :, :]
    return drawn.reshape(BRANCHES, HQ * HD).astype(jnp.bfloat16)


def draw_prefix_keys(key, part):
    drawn = jnp.clip(jax.random.normal(jax.random.fold_in(key, 21), (PREFIX, KVH * HD), jnp.float32), -4.0, 4.0) * 2.5
    return drawn.astype(jnp.bfloat16)


def draw_suffix_keys(key, part):
    suffix_dir = shared_directions(key)
    noise = jnp.clip(jax.random.normal(jax.random.fold_in(key, 31), (BRANCHES, SUF, KVH, HD), jnp.float32), -4.0, 4.0)
    drawn = noise + suffix_dir[None, None, :, :]
    return drawn.reshape(BRANCHES, SUF, KVH * HD).astype(jnp.bfloat16)


def draw_new_keys(key, part):
    suffix_dir = shared_directions(key)
    noise = jnp.clip(jax.random.normal(jax.random.fold_in(key, 41), (BRANCHES, KVH, HD), jnp.float32), -4.0, 4.0)
    drawn = noise + suffix_dir[None, :, :]
    return drawn.reshape(BRANCHES, KVH * HD).astype(jnp.bfloat16)


def draw_fork_list(key, part):
    choose = jax.random.randint(jax.random.fold_in(key, 51), (FORKS,), 0, BR_DEV)
    starts = jnp.arange(FORKS, dtype=jnp.int32) * BR_DEV
    parents = starts + choose
    offsets = (choose[:, None] + 1 + jnp.arange(BR_DEV - 1, dtype=jnp.int32)[None, :]) % BR_DEV
    others = (starts[:, None] + offsets).reshape(-1)
    order = jax.random.permutation(jax.random.fold_in(key, 52), others.shape[0])
    children = others[order[0:FORKS]]
    return jnp.stack([parents, children], axis=1).astype(jnp.int32)


def plant(entries, own_key, least, top_value):
    longest = entries.shape.index(max(entries.shape))
    spots = []
    for shift in (0, 1):
        where = [jax.random.randint(jax.random.fold_in(own_key, axis), (), 0, length) for axis, length in enumerate(entries.shape)]
        where[longest] = (where[longest] + shift) % entries.shape[longest]
        spots.append(tuple(where))
    return entries.at[spots[0]].set(least).at[spots[1]].set(top_value)


def levels(key, shape, pieces, smallest, largest):
    def one(position, parts):
        steps = jax.random.uniform(jax.random.fold_in(jax.random.fold_in(key, 6), position), (parts,), jnp.float32, smallest / len(pieces), largest / len(pieces))
        return jnp.repeat(jnp.exp(steps), shape[position] // parts).reshape((-1,) + (1,) * (len(shape) - position - 1))

    level = one(*pieces[0])
    for cut in pieces[1:]:
        level = level * one(*cut)
    return level


def centred(stream_key, dims, spread, limit, split=(), kind=jnp.bfloat16):
    gain = levels(stream_key, dims, split, -0.22, 0.18) if split else 1.0
    entries = jax.random.normal(stream_key, dims, jnp.float32) * spread * gain
    return jnp.minimum(jnp.maximum(entries, -limit), limit).astype(kind)


def setup_inputs(seed: int = 0, part: int = 0) -> dict:
    arg_keys = jax.random.split(jax.random.key(seed), 10)
    part_keys = jax.random.split(jax.random.fold_in(arg_keys[9], part), 10)
    queries = draw_queries(jax.random.fold_in(jax.random.fold_in(arg_keys[9], part), 71), part)
    prefix_keys = draw_prefix_keys(jax.random.fold_in(jax.random.fold_in(arg_keys[9], part), 71), part)
    prefix_values = centred(part_keys[2], (PREFIX, KVH * HD), 1.0, 6.0, ((0, 8), (1, 2)))
    suffix_keys = draw_suffix_keys(jax.random.fold_in(jax.random.fold_in(arg_keys[9], part), 71), part)
    suffix_values = centred(part_keys[4], (BRANCHES, SUF, KVH * HD), 1.0, 6.0, ((0, 8), (2, 2)))
    new_keys = draw_new_keys(jax.random.fold_in(jax.random.fold_in(arg_keys[9], part), 71), part)
    new_values = centred(part_keys[6], (BRANCHES, KVH * HD), 1.0, 6.0, ((0, 8), (1, 2)))
    suffix_lengths = plant(jax.random.randint(part_keys[7], (BRANCHES,), 0, SUF), jax.random.fold_in(part_keys[7], 1), 0, SUF - 1).astype(jnp.int32)
    fork_list = draw_fork_list(jax.random.fold_in(jax.random.fold_in(arg_keys[9], part), 71), part)
    return {"queries": queries, "prefix_keys": prefix_keys, "prefix_values": prefix_values, "suffix_keys": suffix_keys, "suffix_values": suffix_values, "new_keys": new_keys, "new_values": new_values, "suffix_lengths": suffix_lengths, "fork_list": fork_list}


def rounded(values):
    return lax.optimization_barrier(values.astype(jnp.bfloat16)).astype(jnp.float32)

def reference(queries, prefix_keys, prefix_values, suffix_keys, suffix_values, new_keys, new_values, suffix_lengths, fork_list):
    groups_per = HQ // KVH
    score_scale = 1.0 / math.sqrt(HD)
    parents = fork_list[:, 0].astype(jnp.int32)
    children = fork_list[:, 1].astype(jnp.int32)
    source = jnp.arange(BRANCHES, dtype=jnp.int32).at[children].set(parents)
    length = suffix_lengths[source]
    slot_ids = jnp.arange(SUF, dtype=jnp.int32)
    write_mask = (slot_ids[None, :] == length[:, None])[:, :, None]
    cache_keys = jnp.where(write_mask, new_keys[:, None, :], suffix_keys[source])
    cache_values = jnp.where(write_mask, new_values[:, None, :], suffix_values[source])
    query_heads = queries.astype(jnp.float32).reshape(BRANCHES, KVH, groups_per, HD)
    shard_keys = prefix_keys.reshape(N_SEQ, PRE_DEV, KVH, HD)
    shard_values = prefix_values.reshape(N_SEQ, PRE_DEV, KVH, HD)

    def shard_step(carry, piece):
        run_max, run_sum, run_total = carry
        key_block, value_block = piece
        scores = jnp.einsum('bkgd,jkd->bkgj', query_heads, key_block.astype(jnp.float32), precision=lax.Precision.HIGHEST) * score_scale
        shard_max = lax.optimization_barrier(jnp.max(scores, axis=-1))
        weights = jnp.exp(scores - shard_max[..., None])
        partial_sum = jnp.einsum('bkgj,jkd->bkgd', rounded(weights), value_block.astype(jnp.float32), precision=lax.Precision.HIGHEST)
        partial_total = lax.optimization_barrier(jnp.sum(weights, axis=-1))
        partial_output = rounded(partial_sum / partial_total[..., None])
        new_max = jnp.maximum(run_max, shard_max)
        old_factor = jnp.exp(run_max - new_max)
        new_factor = jnp.exp(shard_max - new_max)
        next_sum = run_sum * old_factor[..., None] + partial_output * (partial_total * new_factor)[..., None]
        next_total = run_total * old_factor + partial_total * new_factor
        return ((new_max, next_sum, next_total), None)
    start_max = jnp.full((BRANCHES, KVH, groups_per), -jnp.inf, jnp.float32)
    start_sum = jnp.zeros((BRANCHES, KVH, groups_per, HD), jnp.float32)
    start_total = jnp.zeros((BRANCHES, KVH, groups_per), jnp.float32)
    (prefix_max, prefix_sum, prefix_total), unused = lax.scan(shard_step, (start_max, start_sum, start_total), (shard_keys, shard_values))
    own_keys = cache_keys.astype(jnp.float32).reshape(BRANCHES, SUF, KVH, HD)
    own_values = cache_values.astype(jnp.float32).reshape(BRANCHES, SUF, KVH, HD)
    scores = jnp.einsum('bkgd,bskd->bkgs', query_heads, own_keys, precision=lax.Precision.HIGHEST) * score_scale
    live = (slot_ids[None, :] <= length[:, None])[:, None, None, :]
    scores = jnp.where(live, scores, -jnp.inf)
    own_max = lax.optimization_barrier(jnp.max(scores, axis=-1))
    weights = jnp.where(live, jnp.exp(scores - own_max[..., None]), 0.0)
    own_sum = jnp.einsum('bkgs,bskd->bkgd', rounded(weights), own_values, precision=lax.Precision.HIGHEST)
    own_total = lax.optimization_barrier(jnp.sum(weights, axis=-1))
    both_max = jnp.maximum(prefix_max, own_max)
    prefix_factor = jnp.exp(prefix_max - both_max)
    own_factor = jnp.exp(own_max - both_max)
    numerator = prefix_sum * prefix_factor[..., None] + own_sum * own_factor[..., None]
    denominator = prefix_total * prefix_factor + own_total * own_factor
    attended = (numerator / denominator[..., None]).reshape(BRANCHES, HQ * HD).astype(jnp.bfloat16)
    return (attended, cache_keys, cache_values)
```

```python
import functools
import math

import jax
import jax.numpy as jnp
from jax import lax
from jax.experimental import pallas as pl
from jax.experimental.pallas import tpu as pltpu
from jax.sharding import PartitionSpec as P

HQ = 40
KVH = 8
HD = 128
GROUP = HQ // KVH
MESH = pl.DeviceIdType.MESH
NT = (((1,), (1,)), ((), ()))
UNROLL_UP_TO = 16
F32 = jnp.float32
BF16 = jnp.bfloat16


def each(start, stop, body):
    if stop - start <= UNROLL_UP_TO:
        for index in range(start, stop):
            body(index)
    else:
        def step(index, carry):
            body(index)
            return carry

        lax.fori_loop(start, stop, step, 0)


def fold(start, stop, body, carry):
    if stop - start <= UNROLL_UP_TO:
        for index in range(start, stop):
            carry = body(index, carry)
        return carry
    return lax.fori_loop(start, stop, body, carry)


def kernel(
    n,
    q_hbm, pk_hbm, pv_hbm, sk_hbm, sv_hbm, nk_hbm, nv_hbm, len_ref, fork_ref,
    att_hbm, ck_hbm, cv_hbm,
    q_in, pk, pv, sk, sv, nk, nv,
    q_f32, q_tiles, pieces, res_out, res_in, lse_out, lse_in, att_rows, att, ck, cv,
    in_sem, out_sem, q_send, q_recv, p_send, p_recv, r_send, r_recv, l_send, l_recv,
):
    me = lax.axis_index("seq")
    branches = q_in.shape[0]
    slots = sk.shape[1]
    kv_local = pk.shape[1] // HD
    rows = q_f32.shape[1]
    used = GROUP * branches
    scale = 1.0 / math.sqrt(HD)
    base = me * branches

    def ahead(k):
        return {"seq": lax.rem(me + k, n)}

    def behind(k):
        return {"seq": lax.rem(me - k + n, n)}

    barrier = pltpu.get_barrier_semaphore()
    each(1, n, lambda k: pl.semaphore_signal(
        barrier, inc=1, device_id=ahead(k), device_id_type=MESH))

    loads = [
        pltpu.make_async_copy(src, dst, in_sem.at[i])
        for i, (src, dst) in enumerate([
            (q_hbm, q_in), (sk_hbm, sk), (sv_hbm, sv), (pk_hbm, pk),
            (pv_hbm, pv), (nk_hbm, nk), (nv_hbm, nv)])
    ]
    for load in loads:
        load.start()

    parent = fork_ref[0, 0] - base
    parent_length = len_ref[0]
    for j in range(1, branches):
        parent_length = jnp.where(parent == j, len_ref[j], parent_length)
    q_f32[...] = jnp.zeros_like(q_f32)
    q_f32[0, used:used + 1, :] = jnp.full((1, HD), fork_ref[0, 1].astype(F32))
    q_f32[0, used + 1:used + 2, :] = jnp.full((1, HD), parent_length.astype(F32))
    loads[0].wait()
    q_all = q_in[...].astype(F32)
    for g in range(kv_local):
        for h in range(GROUP):
            at = (g * GROUP + h) * HD
            q_f32[g, h * branches:(h + 1) * branches, :] = q_all[:, at:at + HD]
    q_tiles[0] = q_f32[...].astype(BF16)

    pl.semaphore_wait(barrier, n - 1)

    def copy(src, dst, send, recv, k, device):
        return pltpu.make_async_remote_copy(
            src_ref=src, dst_ref=dst, send_sem=send.at[k], recv_sem=recv.at[k],
            device_id=device, device_id_type=MESH)

    def q_copy(k):
        return copy(q_tiles.at[0], q_tiles.at[k], q_send, q_recv, k, ahead(k))

    def p_copy(k):
        return copy(pieces.at[0], pieces.at[k], p_send, p_recv, k, ahead(k))

    def r_copy(k):
        return copy(res_out.at[k], res_in.at[k], r_send, r_recv, k, behind(k))

    def l_copy(k):
        return copy(lse_out.at[k], lse_in.at[k], l_send, l_recv, k, behind(k))

    each(1, n, lambda k: q_copy(k).start())

    loads[1].wait()
    loads[2].wait()

    def own_suffix(j):
        return jnp.concatenate([sk[j].astype(F32), sv[j].astype(F32)], axis=0)

    parent_b = jnp.full((2 * slots, sk.shape[2]), parent.astype(F32))
    piece = own_suffix(0)
    for j in range(1, branches):
        piece = jnp.where(parent_b == float(j), own_suffix(j), piece)
    pieces[0] = piece.astype(BF16)
    each(1, n, lambda k: p_copy(k).start())

    loads[3].wait()
    loads[4].wait()
    each(1, n, lambda k: q_copy(k).wait_recv())

    chunk = math.gcd(n, 8)
    lane = lax.broadcasted_iota(jnp.int32, (chunk * rows, HD), 1)

    def block(index):
        first = index * chunk
        top = jnp.zeros((chunk * rows, HD), F32)
        total = jnp.ones((chunk * rows, HD), F32)
        for g in range(kv_local):
            columns = slice(g * HD, (g + 1) * HD)
            q = q_tiles[pl.ds(first, chunk), g].reshape(chunk * rows, HD)
            scores = lax.dot_general(q, pk[:, columns], NT, preferred_element_type=F32) * scale
            row_max = jnp.max(scores, axis=1, keepdims=True)
            weights = jnp.exp(scores - row_max)
            row_total = jnp.sum(weights, axis=1, keepdims=True)
            summed = jnp.dot(weights.astype(BF16), pv[:, columns], preferred_element_type=F32)
            output = (summed / row_total).astype(BF16)
            res_out[pl.ds(first, chunk), g] = output.reshape(chunk, rows, HD)
            top = jnp.where(lane == g, row_max, top)
            total = jnp.where(lane == g, row_total, total)
        lse_out[pl.ds(first, chunk)] = (top + jnp.log(total)).reshape(chunk, rows, HD)

    each(0, n // chunk, block)

    def send_back(k):
        r_copy(k).start()
        l_copy(k).start()

    each(1, n, send_back)

    each(1, n, lambda k: p_copy(k).wait_recv())
    loads[5].wait()
    loads[6].wait()
    blocks = sk.shape[2] // HD

    def wide(row):
        return jnp.concatenate([jnp.broadcast_to(row, (2 * slots, HD))] * blocks, axis=1)

    def land(k, carry):
        notes = q_tiles[k, 0].astype(F32)
        child = wide(notes[used:used + 1])
        child_length = wide(notes[used + 1:used + 2])
        arrived = pieces[k].astype(F32)
        out = []
        for j in range(branches):
            cache, length = carry[j]
            mine = child == (base + j).astype(F32)
            out.append((jnp.where(mine, arrived, cache), jnp.where(mine, child_length, length)))
        return tuple(out)

    shape = (2 * slots, sk.shape[2])
    landed = fold(0, n, land, tuple(
        (own_suffix(j), jnp.full(shape, len_ref[j].astype(F32))) for j in range(branches)))

    slot = lax.rem(lax.broadcasted_iota(jnp.int32, shape, 0), slots).astype(F32)
    nk_all, nv_all = nk[...].astype(F32), nv[...].astype(F32)
    caches = []
    for j in range(branches):
        cache, length = landed[j]
        fresh = jnp.concatenate([
            jnp.broadcast_to(nk_all[j:j + 1], (slots, shape[1])),
            jnp.broadcast_to(nv_all[j:j + 1], (slots, shape[1]))], axis=0)
        cache = jnp.where(slot == length, fresh, cache)
        ck[j] = cache[:slots].astype(BF16)
        cv[j] = cache[slots:].astype(BF16)
        caches.append(cache)
    stores = [
        pltpu.make_async_copy(ck, ck_hbm, out_sem.at[0]),
        pltpu.make_async_copy(cv, cv_hbm, out_sem.at[1]),
    ]
    for store in stores:
        store.start()

    count = branches * slots
    row_id = lax.broadcasted_iota(jnp.int32, (rows, count), 0)
    key_id = lax.broadcasted_iota(jnp.int32, (rows, count), 1)
    key_length = landed[0][1][:1, :count]
    for j in range(1, branches):
        key_length = jnp.where(key_id[:1] >= j * slots, landed[j][1][:1, :count], key_length)
    live = jnp.logical_and(
        lax.rem(row_id, branches) == key_id // slots,
        lax.rem(key_id, slots).astype(F32) <= jnp.broadcast_to(key_length, (rows, count)))
    lane = lax.broadcasted_iota(jnp.int32, (rows, HD), 1)
    own_top = jnp.zeros((rows, HD), F32)
    own_total = jnp.ones((rows, HD), F32)
    own_sums = []
    for g in range(kv_local):
        columns = slice(g * HD, (g + 1) * HD)
        keys = jnp.concatenate([c[:slots, columns] for c in caches], axis=0).astype(BF16)
        values = jnp.concatenate([c[slots:, columns] for c in caches], axis=0).astype(BF16)
        scores = lax.dot_general(q_tiles[0, g], keys, NT, preferred_element_type=F32) * scale
        row_max = jnp.max(jnp.where(live, scores, -jnp.inf), axis=1, keepdims=True)
        weights = jnp.where(live, jnp.exp(scores - row_max), 0.0)
        row_total = jnp.sum(weights, axis=1, keepdims=True)
        own_sums.append(jnp.dot(weights.astype(BF16), values, preferred_element_type=F32))
        own_top = jnp.where(lane == g, row_max, own_top)
        own_total = jnp.where(lane == g, row_total, own_total)

    def arrive(k):
        l_copy(k).wait_recv()
        r_copy(k).wait_recv()

    each(1, n, arrive)
    best = fold(1, n, lambda k, m: jnp.maximum(m, lse_in[k]), jnp.maximum(own_top, lse_out[0]))

    def add(factor, output, carry):
        sums, total = carry
        sums = tuple(
            s + output[g].astype(F32) * factor[:, g:g + 1] for g, s in enumerate(sums))
        return sums, total + factor

    own_factor = jnp.exp(own_top - best)
    carry = (
        tuple(s * own_factor[:, g:g + 1] for g, s in enumerate(own_sums)),
        own_total * own_factor)
    carry = add(jnp.exp(lse_out[0] - best), res_out.at[0], carry)
    sums, total = fold(
        1, n, lambda k, c: add(jnp.exp(lse_in[k] - best), res_in.at[k], c), carry)
    for g in range(kv_local):
        att_rows[g] = sums[g] / total[:, g:g + 1]
    att[...] = jnp.concatenate(
        [att_rows[g, h * branches:(h + 1) * branches, :]
         for g in range(kv_local) for h in range(GROUP)], axis=1).astype(BF16)
    stores.append(pltpu.make_async_copy(att, att_hbm, out_sem.at[2]))
    stores[2].start()

    def drain(k):
        q_copy(k).wait_send()
        p_copy(k).wait_send()
        r_copy(k).wait_send()
        l_copy(k).wait_send()

    each(1, n, drain)
    for store in stores:
        store.wait()


def shards(n, *args):
    queries, prefix_keys, prefix_values, suffix_keys, suffix_values = args[:5]
    new_keys, new_values, suffix_lengths, fork_list = args[5:]
    branches = queries.shape[0]
    slots, width = suffix_keys.shape[1:]
    kv_local = width // HD
    rows = -(-(GROUP * branches + 2) // 16) * 16
    assert fork_list.shape[0] == 1 and n * branches <= 256
    dma = pltpu.SemaphoreType.DMA
    any_spec = pl.BlockSpec(memory_space=pl.ANY)
    smem_spec = pl.BlockSpec(memory_space=pltpu.SMEM)
    like = lambda x: pltpu.VMEM(x.shape, x.dtype)
    return pl.pallas_call(
        functools.partial(kernel, n),
        out_shape=(
            jax.ShapeDtypeStruct(queries.shape, BF16),
            jax.ShapeDtypeStruct(suffix_keys.shape, BF16),
            jax.ShapeDtypeStruct(suffix_values.shape, BF16),
        ),
        in_specs=[any_spec] * 7 + [smem_spec] * 2,
        out_specs=(any_spec,) * 3,
        scratch_shapes=[
            like(queries), like(prefix_keys), like(prefix_values), like(suffix_keys),
            like(suffix_values), like(new_keys), like(new_values),
            pltpu.VMEM((kv_local, rows, HD), F32),
            pltpu.VMEM((n, kv_local, rows, HD), BF16),
            pltpu.VMEM((n, 2 * slots, width), BF16),
            pltpu.VMEM((n, kv_local, rows, HD), BF16),
            pltpu.VMEM((n, kv_local, rows, HD), BF16),
            pltpu.VMEM((n, rows, HD), F32),
            pltpu.VMEM((n, rows, HD), F32),
            pltpu.VMEM((kv_local, rows, HD), F32),
            like(queries), like(suffix_keys), like(suffix_values),
            dma((7,)), dma((3,)),
        ] + [dma((n,))] * 8,
        compiler_params=pltpu.CompilerParams(
            collective_id=0, has_side_effects=True, vmem_limit_bytes=32 * 2**20),
    )(*args)


def solution(mesh):
    return jax.shard_map(
        functools.partial(shards, mesh.shape["seq"]),
        mesh=mesh,
        in_specs=(
            P(("groups", "seq"), "mp"),
            P(("groups", "seq"), "mp"),
            P(("groups", "seq"), "mp"),
            P(("groups", "seq"), None, "mp"),
            P(("groups", "seq"), None, "mp"),
            P(("groups", "seq"), "mp"),
            P(("groups", "seq"), "mp"),
            P(("groups", "seq")),
            P(("groups", "seq"), None),
        ),
        out_specs=(
            P(("groups", "seq"), "mp"),
            P(("groups", "seq"), None, "mp"),
            P(("groups", "seq"), None, "mp"),
        ),
        check_vma=False,
    )
```

```python
import functools
import math

import jax
import jax.numpy as jnp
from jax import lax
from jax.experimental import pallas as pl
from jax.experimental.pallas import tpu as pltpu
from jax.sharding import PartitionSpec as P

HQ = 40
KVH = 8
HD = 128
GROUP = HQ // KVH
BRANCHES = 2
TILE = 8
MESH = pl.DeviceIdType.MESH
NT = (((1,), (1,)), ((), ()))
UNROLL_UP_TO = 16
F32 = jnp.float32
BF16 = jnp.bfloat16


def each(start, stop, body):
    if stop - start <= UNROLL_UP_TO:
        for index in range(start, stop):
            body(index)
    else:
        def step(index, carry):
            body(index)
            return carry

        lax.fori_loop(start, stop, step, 0)


def fold(start, stop, body, carry):
    if stop - start <= UNROLL_UP_TO:
        for index in range(start, stop):
            carry = body(index, carry)
        return carry
    return lax.fori_loop(start, stop, body, carry)


def kernel(
    n,
    q_hbm, pk_hbm, pv_hbm, sk_hbm, sv_hbm, nk_hbm, nv_hbm, len_ref, fork_ref,
    att, ck, cv,
    q_in, pk, pv, sk, sv, nk, nv,
    q_f32, q_tiles, pieces, res_out, res_in, att_rows,
    in_sem, q_send, q_recv, p_send, p_recv, r_send, r_recv,
):
    me = lax.axis_index("seq")
    slots = sk.shape[1]
    kv_local = pk.shape[1] // HD
    scale = 1.0 / math.sqrt(HD)
    base = me * BRANCHES
    rest = kv_local * TILE
    notes_at = rest + TILE
    chunk = math.gcd(n, 4)

    def partner(k):
        other, bit = me, 1
        while bit < n:
            other = other + (k // bit) % 2 * bit * (1 - 2 * ((me // bit) % 2))
            bit *= 2
        return {"seq": other}

    barrier = pltpu.get_barrier_semaphore()
    each(1, n, lambda k: pl.semaphore_signal(
        barrier, inc=1, device_id=partner(k), device_id_type=MESH))

    loads = [
        pltpu.make_async_copy(src, dst, in_sem.at[i])
        for i, (src, dst) in enumerate([
            (q_hbm, q_in), (sk_hbm, sk), (sv_hbm, sv), (pk_hbm, pk),
            (pv_hbm, pv), (nk_hbm, nk), (nv_hbm, nv)])
    ]
    for load in loads:
        load.start()

    def row_of(g, h):
        return g * TILE + h * BRANCHES if h < GROUP - 1 else rest + g * BRANCHES

    parent = fork_ref[0, 0] - base
    parent_length = jnp.where(parent == 0, len_ref[0], len_ref[1])
    q_f32[notes_at:] = jnp.zeros((TILE, HD), F32)
    q_f32[notes_at:notes_at + 1] = jnp.full((1, HD), fork_ref[0, 1].astype(F32))
    q_f32[notes_at + 1:notes_at + 2] = jnp.full((1, HD), parent_length.astype(F32))
    loads[0].wait()
    q_all = q_in[...].astype(F32)
    for g in range(kv_local):
        for h in range(GROUP):
            at = (g * GROUP + h) * HD
            q_f32[row_of(g, h):row_of(g, h) + BRANCHES, :] = q_all[:, at:at + HD]
    q_tiles[0] = q_f32[...].astype(BF16)

    pl.semaphore_wait(barrier, n - 1)

    def copy(src, dst, send, recv, k):
        return pltpu.make_async_remote_copy(
            src_ref=src, dst_ref=dst, send_sem=send.at[k], recv_sem=recv.at[k],
            device_id=partner(k), device_id_type=MESH)

    def q_copy(k):
        return copy(q_tiles.at[0], q_tiles.at[k], q_send, q_recv, k)

    def p_copy(k):
        return copy(pieces.at[0], pieces.at[k], p_send, p_recv, k)

    def r_copy(k):
        return copy(res_out.at[k], res_in.at[k], r_send, r_recv, k)

    def far_first(body):
        each(chunk, n, body)
        each(1, chunk, body)

    far_first(lambda k: q_copy(k).start())

    loads[1].wait()
    loads[2].wait()

    def own_suffix(j):
        return jnp.concatenate([sk[j].astype(F32), sv[j].astype(F32)], axis=0)

    parent_b = jnp.full((2 * slots, sk.shape[2]), parent.astype(F32))
    pieces[0] = jnp.where(parent_b == 0.0, own_suffix(0), own_suffix(1)).astype(BF16)
    far_first(lambda k: p_copy(k).start())

    loads[3].wait()
    loads[4].wait()

    count = chunk * TILE
    lane = lax.rem(lax.broadcasted_iota(jnp.int32, (count, HD), 1), 16)
    owner_s = lax.rem(lax.broadcasted_iota(jnp.int32, (count, pk.shape[0]), 0), TILE) // BRANCHES
    owner_o = lax.rem(lax.broadcasted_iota(jnp.int32, (count, HD), 0), TILE) // BRANCHES

    def softmax(scores):
        row_max = jnp.max(scores, axis=1, keepdims=True)
        weights = jnp.exp(scores - row_max)
        return row_max, jnp.sum(weights, axis=1, keepdims=True), weights.astype(BF16)

    def block(first):
        tiles = q_tiles[pl.ds(first, chunk)].astype(F32)

        def rows(at):
            return tiles[:, at:at + TILE].reshape(count, HD)

        last = rows(rest)
        scores, rest_scores = [], None
        for g in range(kv_local):
            q = jnp.concatenate([rows(g * TILE), last], axis=0).astype(BF16)
            s = lax.dot_general(
                q, pk[:, g * HD:(g + 1) * HD], NT, preferred_element_type=F32) * scale
            scores.append(s[:count])
            rest_scores = s[count:] if g == 0 else jnp.where(owner_s == g, s[count:], rest_scores)
        outputs = []
        top = jnp.zeros((count, HD), F32)
        total = jnp.ones((count, HD), F32)
        for g, s in enumerate(scores + [rest_scores]):
            row_max, row_total, weights = softmax(s)
            if g < kv_local:
                summed = jnp.dot(
                    weights, pv[:, g * HD:(g + 1) * HD], preferred_element_type=F32)
            else:
                every = jnp.dot(weights, pv[...], preferred_element_type=F32)
                summed = every[:, :HD]
                for i in range(1, kv_local):
                    summed = jnp.where(owner_o == i, every[:, i * HD:(i + 1) * HD], summed)
            outputs.append(summed * (1.0 / row_total))
            top = jnp.where(lane == g, row_max, top)
            total = jnp.where(lane == g, row_total, total)
        lse = top + jnp.log(total)
        high = lse.astype(BF16).astype(F32)
        middle = (lse - high).astype(BF16).astype(F32)
        low = lse - high - middle
        at = lax.broadcasted_iota(jnp.int32, (count, HD), 1) // 16
        outputs.append(jnp.where(at == 0, high, jnp.where(at == 1, middle, low)))
        res_out[pl.ds(first, chunk)] = jnp.concatenate(
            [o.reshape(chunk, TILE, HD) for o in outputs], axis=1).astype(BF16)

    each(1, chunk, lambda k: q_copy(k).wait_recv())
    block(0)
    each(1, chunk, lambda k: r_copy(k).start())

    def far_block(index):
        first = index * chunk
        each(0, chunk, lambda i: q_copy(first + i).wait_recv())
        block(first)
        each(0, chunk, lambda i: r_copy(first + i).start())

    each(1, n // chunk, far_block)

    each(1, n, lambda k: p_copy(k).wait_recv())
    loads[5].wait()
    loads[6].wait()
    blocks = sk.shape[2] // HD

    def wide(row):
        return jnp.concatenate([jnp.broadcast_to(row, (2 * slots, HD))] * blocks, axis=1)

    def land(k, carry):
        notes = q_tiles[k].astype(F32)[notes_at:]
        child, child_length = wide(notes[:1]), wide(notes[1:2])
        arrived = pieces[k].astype(F32)
        out = []
        for j in range(BRANCHES):
            cache, length = carry[j]
            mine = child == (base + j).astype(F32)
            out.append((jnp.where(mine, arrived, cache), jnp.where(mine, child_length, length)))
        return tuple(out)

    shape = (2 * slots, sk.shape[2])
    landed = fold(0, n, land, tuple(
        (own_suffix(j), jnp.full(shape, len_ref[j].astype(F32))) for j in range(BRANCHES)))

    slot = lax.rem(lax.broadcasted_iota(jnp.int32, shape, 0), slots).astype(F32)
    nk_all, nv_all = nk[...].astype(F32), nv[...].astype(F32)
    caches = []
    for j in range(BRANCHES):
        cache, length = landed[j]
        fresh = jnp.concatenate([
            jnp.broadcast_to(nk_all[j:j + 1], (slots, shape[1])),
            jnp.broadcast_to(nv_all[j:j + 1], (slots, shape[1]))], axis=0)
        cache = jnp.where(slot == length, fresh, cache)
        ck[j] = cache[:slots].astype(BF16)
        cv[j] = cache[slots:].astype(BF16)
        caches.append(cache)

    parts = kv_local + 1
    keys_count = BRANCHES * slots
    row_id = lax.broadcasted_iota(jnp.int32, (parts * TILE, keys_count), 0)
    key_id = lax.broadcasted_iota(jnp.int32, (parts * TILE, keys_count), 1)
    key_length = jnp.where(
        key_id[:1] >= slots, landed[1][1][:1, :keys_count], landed[0][1][:1, :keys_count])
    live = jnp.logical_and(
        lax.rem(row_id, BRANCHES) == key_id // slots,
        lax.rem(key_id, slots).astype(F32) <= jnp.broadcast_to(key_length, row_id.shape))
    own_q = q_f32[...]
    own_scores, rest_scores = [], None
    owner = lax.broadcasted_iota(jnp.int32, (TILE, HD), 0) // BRANCHES
    for g in range(kv_local):
        keys = jnp.concatenate(
            [c[:slots, g * HD:(g + 1) * HD] for c in caches], axis=0).astype(BF16)
        q = jnp.concatenate(
            [own_q[g * TILE:(g + 1) * TILE], own_q[rest:notes_at]], axis=0).astype(BF16)
        s = lax.dot_general(q, keys, NT, preferred_element_type=F32) * scale
        own_scores.append(s[:TILE])
        rest_scores = s[TILE:] if g == 0 else jnp.where(
            owner[:, :keys_count] == g, s[TILE:], rest_scores)
    scores = jnp.concatenate(own_scores + [rest_scores], axis=0)
    row_max = jnp.max(jnp.where(live, scores, -jnp.inf), axis=1, keepdims=True)
    weights = jnp.where(live, jnp.exp(scores - row_max), 0.0)
    row_total = jnp.sum(weights, axis=1, keepdims=True)
    own_sums, rest_sum = [], None
    for g in range(kv_local):
        values = jnp.concatenate(
            [c[slots:, g * HD:(g + 1) * HD] for c in caches], axis=0).astype(BF16)
        w = jnp.concatenate(
            [weights[g * TILE:(g + 1) * TILE], weights[rest:notes_at]], axis=0).astype(BF16)
        o = jnp.dot(w, values, preferred_element_type=F32)
        own_sums.append(o[:TILE])
        rest_sum = o[TILE:] if g == 0 else jnp.where(owner == g, o[TILE:], rest_sum)
    own_sums.append(rest_sum)
    lane = lax.broadcasted_iota(jnp.int32, (TILE, HD), 1)
    own_top = jnp.zeros((TILE, HD), F32)
    own_total = jnp.ones((TILE, HD), F32)
    for g in range(parts):
        at = slice(g * TILE, (g + 1) * TILE)
        own_top = jnp.where(lane == g, row_max[at], own_top)
        own_total = jnp.where(lane == g, row_total[at], own_total)

    def lse_of(tile):
        terms = tile.astype(F32)[notes_at:]
        return terms + pltpu.roll(terms, HD - 16, 1) + pltpu.roll(terms, HD - 32, 1)

    each(1, n, lambda k: r_copy(k).wait_recv())
    best = fold(
        1, n, lambda k, m: jnp.maximum(m, lse_of(res_in[k])),
        jnp.maximum(own_top, lse_of(res_out[0])))

    def add(tile, carry):
        sums, total = carry
        factor = jnp.exp(lse_of(tile) - best)
        tile = tile.astype(F32)
        sums = tuple(
            s + tile[g * TILE:(g + 1) * TILE] * factor[:, g:g + 1] for g, s in enumerate(sums))
        return sums, total + factor

    own_factor = jnp.exp(own_top - best)
    carry = (
        tuple(s * own_factor[:, g:g + 1] for g, s in enumerate(own_sums)),
        own_total * own_factor)
    carry = add(res_out[0], carry)
    sums, total = fold(1, n, lambda k, c: add(res_in[k], c), carry)
    for g in range(parts):
        att_rows[g * TILE:(g + 1) * TILE, :] = sums[g] / total[:, g:g + 1]
    att[...] = jnp.concatenate(
        [att_rows[row_of(g, h):row_of(g, h) + BRANCHES, :]
         for g in range(kv_local) for h in range(GROUP)], axis=1).astype(BF16)

    def drain(k):
        q_copy(k).wait_send()
        p_copy(k).wait_send()
        r_copy(k).wait_send()

    each(1, n, drain)


def place(*refs):
    count = len(refs) // 2
    sems = refs[-1]
    copies = [
        pltpu.make_async_copy(refs[i], refs[count + i], sems.at[i]) for i in range(count)]
    for item in copies:
        item.start()
    for item in copies:
        item.wait()


def shards(n, *args):
    queries, prefix_keys, prefix_values, suffix_keys, suffix_values = args[:5]
    new_keys, new_values, suffix_lengths, fork_list = args[5:]
    slots, width = suffix_keys.shape[1:]
    kv_local = width // HD
    rows = (kv_local + 2) * TILE
    assert queries.shape[0] == BRANCHES and fork_list.shape[0] == 1
    assert n * BRANCHES <= 256 and rows % 16 == 0 and n & (n - 1) == 0
    dma = pltpu.SemaphoreType.DMA
    hbm_spec = pl.BlockSpec(memory_space=pltpu.HBM)
    smem_spec = pl.BlockSpec(memory_space=pltpu.SMEM)
    vmem_spec = pl.BlockSpec(memory_space=pltpu.VMEM)
    like = lambda x: pltpu.VMEM(x.shape, x.dtype)
    out_shape = (
        jax.ShapeDtypeStruct(queries.shape, BF16),
        jax.ShapeDtypeStruct(suffix_keys.shape, BF16),
        jax.ShapeDtypeStruct(suffix_values.shape, BF16),
    )
    results = pl.pallas_call(
        functools.partial(kernel, n),
        out_shape=out_shape,
        in_specs=[hbm_spec] * 7 + [smem_spec] * 2,
        out_specs=(vmem_spec,) * 3,
        scratch_shapes=[
            like(queries), like(prefix_keys), like(prefix_values), like(suffix_keys),
            like(suffix_values), like(new_keys), like(new_values),
            pltpu.VMEM((rows, HD), F32),
            pltpu.VMEM((n, rows, HD), BF16),
            pltpu.VMEM((n, 2 * slots, width), BF16),
            pltpu.VMEM((n, rows, HD), BF16),
            pltpu.VMEM((n, rows, HD), BF16),
            pltpu.VMEM((rows, HD), F32),
            dma((7,)),
        ] + [dma((n,))] * 6,
        compiler_params=pltpu.CompilerParams(
            collective_id=0, has_side_effects=True, vmem_limit_bytes=64 * 2**20),
    )(*args)
    return pl.pallas_call(
        place,
        out_shape=out_shape,
        in_specs=[hbm_spec] * 3,
        out_specs=(hbm_spec,) * 3,
        scratch_shapes=[dma((3,))],
        compiler_params=pltpu.CompilerParams(vmem_limit_bytes=64 * 2**20),
    )(*results)


def solution(mesh):
    return jax.shard_map(
        functools.partial(shards, mesh.shape["seq"]),
        mesh=mesh,
        in_specs=(
            P(("groups", "seq"), "mp"),
            P(("groups", "seq"), "mp"),
            P(("groups", "seq"), "mp"),
            P(("groups", "seq"), None, "mp"),
            P(("groups", "seq"), None, "mp"),
            P(("groups", "seq"), "mp"),
            P(("groups", "seq"), "mp"),
            P(("groups", "seq")),
            P(("groups", "seq"), None),
        ),
        out_specs=(
            P(("groups", "seq"), "mp"),
            P(("groups", "seq"), None, "mp"),
            P(("groups", "seq"), None, "mp"),
        ),
        check_vma=False,
    )
```

```python
import functools
import math

import jax
import jax.numpy as jnp
from jax import lax
from jax.experimental import pallas as pl
from jax.experimental.pallas import tpu as pltpu
from jax.sharding import PartitionSpec as P

HQ = 40
KVH = 8
HD = 128
GROUP = HQ // KVH
BRANCHES = 2
TILE = 8
MESH = pl.DeviceIdType.MESH
NT = (((1,), (1,)), ((), ()))
UNROLL_UP_TO = 16
F32 = jnp.float32
BF16 = jnp.bfloat16


def each(start, stop, body):
    if stop - start <= UNROLL_UP_TO:
        for index in range(start, stop):
            body(index)
    else:
        def step(index, carry):
            body(index)
            return carry

        lax.fori_loop(start, stop, step, 0)


def fold(start, stop, body, carry):
    if stop - start <= UNROLL_UP_TO:
        for index in range(start, stop):
            carry = body(index, carry)
        return carry
    return lax.fori_loop(start, stop, body, carry)


def kernel(
    n,
    q_hbm, pk_hbm, pv_hbm, sk_hbm, sv_hbm, nk_hbm, nv_hbm, len_hbm, fork_hbm,
    att, ck, cv,
    q_in, pk, pv, sk, sv, nk, nv, len_ref, fork_ref,
    q_f32, q_tiles, pieces, res_out, res_in, att_rows,
    in_sem, q_send, q_recv, p_send, p_recv, r_send, r_recv,
):
    me = lax.axis_index("seq")
    slots = sk.shape[1]
    kv_local = pk.shape[1] // HD
    scale = 1.0 / math.sqrt(HD)
    base = me * BRANCHES
    rest = kv_local * TILE
    notes_at = rest + TILE
    chunk = math.gcd(n, 4)

    def partner(k):
        other, bit = me, 1
        while bit < n:
            other = other + (k // bit) % 2 * bit * (1 - 2 * ((me // bit) % 2))
            bit *= 2
        return {"seq": other}

    barrier = pltpu.get_barrier_semaphore()
    each(1, n, lambda k: pl.semaphore_signal(
        barrier, inc=1, device_id=partner(k), device_id_type=MESH))

    loads = [
        pltpu.make_async_copy(src, dst, in_sem.at[i])
        for i, (src, dst) in enumerate([
            (q_hbm, q_in), (sk_hbm, sk), (sv_hbm, sv), (pk_hbm, pk),
            (pv_hbm, pv), (nk_hbm, nk), (nv_hbm, nv), (len_hbm, len_ref), (fork_hbm, fork_ref)])
    ]
    for i in (0, 7, 8, 1, 2, 3, 4, 5, 6):
        loads[i].start()

    def row_of(g, h):
        return g * TILE + h * BRANCHES if h < GROUP - 1 else rest + g * BRANCHES

    loads[7].wait()
    loads[8].wait()
    parent = fork_ref[0, 0] - base
    parent_length = jnp.where(parent == 0, len_ref[0], len_ref[1])
    q_f32[notes_at:] = jnp.zeros((TILE, HD), F32)
    q_f32[notes_at:notes_at + 1] = jnp.full((1, HD), fork_ref[0, 1].astype(F32))
    q_f32[notes_at + 1:notes_at + 2] = jnp.full((1, HD), parent_length.astype(F32))
    loads[0].wait()
    q_all = q_in[...].astype(F32)
    for g in range(kv_local):
        for h in range(GROUP):
            at = (g * GROUP + h) * HD
            q_f32[row_of(g, h):row_of(g, h) + BRANCHES, :] = q_all[:, at:at + HD]
    q_tiles[0] = q_f32[...].astype(BF16)

    pl.semaphore_wait(barrier, n - 1)

    def copy(src, dst, send, recv, k):
        return pltpu.make_async_remote_copy(
            src_ref=src, dst_ref=dst, send_sem=send.at[k], recv_sem=recv.at[k],
            device_id=partner(k), device_id_type=MESH)

    def q_copy(k):
        return copy(q_tiles.at[0], q_tiles.at[k], q_send, q_recv, k)

    def p_copy(k):
        return copy(pieces.at[0], pieces.at[k], p_send, p_recv, k)

    def r_copy(k):
        return copy(res_out.at[k], res_in.at[k], r_send, r_recv, k)

    def far_first(body):
        each(chunk, n, body)
        each(1, chunk, body)

    far_first(lambda k: q_copy(k).start())

    loads[1].wait()
    loads[2].wait()

    def own_suffix(j):
        return jnp.concatenate([sk[j].astype(F32), sv[j].astype(F32)], axis=0)

    parent_b = jnp.full((2 * slots, sk.shape[2]), parent.astype(F32))
    pieces[0] = jnp.where(parent_b == 0.0, own_suffix(0), own_suffix(1)).astype(BF16)
    far_first(lambda k: p_copy(k).start())

    loads[3].wait()
    loads[4].wait()

    count = chunk * TILE
    lane = lax.rem(lax.broadcasted_iota(jnp.int32, (count, HD), 1), 16)
    owner_s = lax.rem(lax.broadcasted_iota(jnp.int32, (count, pk.shape[0]), 0), TILE) // BRANCHES
    owner_o = lax.rem(lax.broadcasted_iota(jnp.int32, (count, HD), 0), TILE) // BRANCHES

    def softmax(scores):
        row_max = jnp.max(scores, axis=1, keepdims=True)
        weights = jnp.exp(scores - row_max)
        return row_max, jnp.sum(weights, axis=1, keepdims=True), weights.astype(BF16)

    def block(first):
        tiles = q_tiles[pl.ds(first, chunk)].astype(F32)

        def rows(at):
            return tiles[:, at:at + TILE].reshape(count, HD)

        last = rows(rest)
        scores, rest_scores = [], None
        for g in range(kv_local):
            q = jnp.concatenate([rows(g * TILE), last], axis=0).astype(BF16)
            s = lax.dot_general(
                q, pk[:, g * HD:(g + 1) * HD], NT, preferred_element_type=F32) * scale
            scores.append(s[:count])
            rest_scores = s[count:] if g == 0 else jnp.where(owner_s == g, s[count:], rest_scores)
        outputs = []
        top = jnp.zeros((count, HD), F32)
        total = jnp.ones((count, HD), F32)
        for g, s in enumerate(scores + [rest_scores]):
            row_max, row_total, weights = softmax(s)
            if g < kv_local:
                summed = jnp.dot(
                    weights, pv[:, g * HD:(g + 1) * HD], preferred_element_type=F32)
            else:
                every = jnp.dot(weights, pv[...], preferred_element_type=F32)
                summed = every[:, :HD]
                for i in range(1, kv_local):
                    summed = jnp.where(owner_o == i, every[:, i * HD:(i + 1) * HD], summed)
            outputs.append(summed * (1.0 / row_total))
            top = jnp.where(lane == g, row_max, top)
            total = jnp.where(lane == g, row_total, total)
        lse = top + jnp.log(total)
        high = lse.astype(BF16).astype(F32)
        middle = (lse - high).astype(BF16).astype(F32)
        low = lse - high - middle
        at = lax.broadcasted_iota(jnp.int32, (count, HD), 1) // 16
        outputs.append(jnp.where(at == 0, high, jnp.where(at == 1, middle, low)))
        res_out[pl.ds(first, chunk)] = jnp.concatenate(
            [o.reshape(chunk, TILE, HD) for o in outputs], axis=1).astype(BF16)

    each(1, chunk, lambda k: q_copy(k).wait_recv())
    block(0)
    each(1, chunk, lambda k: r_copy(k).start())

    def far_block(index):
        first = index * chunk
        each(0, chunk, lambda i: q_copy(first + i).wait_recv())
        block(first)
        each(0, chunk, lambda i: r_copy(first + i).start())

    each(1, n // chunk, far_block)

    each(1, n, lambda k: p_copy(k).wait_recv())
    loads[5].wait()
    loads[6].wait()
    blocks = sk.shape[2] // HD

    def wide(row):
        return jnp.concatenate([jnp.broadcast_to(row, (2 * slots, HD))] * blocks, axis=1)

    def land(k, carry):
        notes = q_tiles[k].astype(F32)[notes_at:]
        child, child_length = wide(notes[:1]), wide(notes[1:2])
        arrived = pieces[k].astype(F32)
        out = []
        for j in range(BRANCHES):
            cache, length = carry[j]
            mine = child == (base + j).astype(F32)
            out.append((jnp.where(mine, arrived, cache), jnp.where(mine, child_length, length)))
        return tuple(out)

    shape = (2 * slots, sk.shape[2])
    landed = fold(0, n, land, tuple(
        (own_suffix(j), jnp.full(shape, len_ref[j].astype(F32))) for j in range(BRANCHES)))

    slot = lax.rem(lax.broadcasted_iota(jnp.int32, shape, 0), slots).astype(F32)
    nk_all, nv_all = nk[...].astype(F32), nv[...].astype(F32)
    caches = []
    for j in range(BRANCHES):
        cache, length = landed[j]
        fresh = jnp.concatenate([
            jnp.broadcast_to(nk_all[j:j + 1], (slots, shape[1])),
            jnp.broadcast_to(nv_all[j:j + 1], (slots, shape[1]))], axis=0)
        cache = jnp.where(slot == length, fresh, cache)
        ck[j] = cache[:slots].astype(BF16)
        cv[j] = cache[slots:].astype(BF16)
        caches.append(cache)

    parts = kv_local + 1
    keys_count = BRANCHES * slots
    row_id = lax.broadcasted_iota(jnp.int32, (parts * TILE, keys_count), 0)
    key_id = lax.broadcasted_iota(jnp.int32, (parts * TILE, keys_count), 1)
    key_length = jnp.where(
        key_id[:1] >= slots, landed[1][1][:1, :keys_count], landed[0][1][:1, :keys_count])
    live = jnp.logical_and(
        lax.rem(row_id, BRANCHES) == key_id // slots,
        lax.rem(key_id, slots).astype(F32) <= jnp.broadcast_to(key_length, row_id.shape))
    own_q = q_f32[...]
    own_scores, rest_scores = [], None
    owner = lax.broadcasted_iota(jnp.int32, (TILE, HD), 0) // BRANCHES
    for g in range(kv_local):
        keys = jnp.concatenate(
            [c[:slots, g * HD:(g + 1) * HD] for c in caches], axis=0).astype(BF16)
        q = jnp.concatenate(
            [own_q[g * TILE:(g + 1) * TILE], own_q[rest:notes_at]], axis=0).astype(BF16)
        s = lax.dot_general(q, keys, NT, preferred_element_type=F32) * scale
        own_scores.append(s[:TILE])
        rest_scores = s[TILE:] if g == 0 else jnp.where(
            owner[:, :keys_count] == g, s[TILE:], rest_scores)
    scores = jnp.concatenate(own_scores + [rest_scores], axis=0)
    row_max = jnp.max(jnp.where(live, scores, -jnp.inf), axis=1, keepdims=True)
    weights = jnp.where(live, jnp.exp(scores - row_max), 0.0)
    row_total = jnp.sum(weights, axis=1, keepdims=True)
    own_sums, rest_sum = [], None
    for g in range(kv_local):
        values = jnp.concatenate(
            [c[slots:, g * HD:(g + 1) * HD] for c in caches], axis=0).astype(BF16)
        w = jnp.concatenate(
            [weights[g * TILE:(g + 1) * TILE], weights[rest:notes_at]], axis=0).astype(BF16)
        o = jnp.dot(w, values, preferred_element_type=F32)
        own_sums.append(o[:TILE])
        rest_sum = o[TILE:] if g == 0 else jnp.where(owner == g, o[TILE:], rest_sum)
    own_sums.append(rest_sum)
    lane = lax.broadcasted_iota(jnp.int32, (TILE, HD), 1)
    own_top = jnp.zeros((TILE, HD), F32)
    own_total = jnp.ones((TILE, HD), F32)
    for g in range(parts):
        at = slice(g * TILE, (g + 1) * TILE)
        own_top = jnp.where(lane == g, row_max[at], own_top)
        own_total = jnp.where(lane == g, row_total[at], own_total)

    def lse_of(tile):
        terms = tile.astype(F32)[notes_at:]
        return terms + pltpu.roll(terms, HD - 16, 1) + pltpu.roll(terms, HD - 32, 1)

    each(1, n, lambda k: r_copy(k).wait_recv())
    best = fold(
        1, n, lambda k, m: jnp.maximum(m, lse_of(res_in[k])),
        jnp.maximum(own_top, lse_of(res_out[0])))

    def add(tile, carry):
        sums, total = carry
        factor = jnp.exp(lse_of(tile) - best)
        tile = tile.astype(F32)
        sums = tuple(
            s + tile[g * TILE:(g + 1) * TILE] * factor[:, g:g + 1] for g, s in enumerate(sums))
        return sums, total + factor

    own_factor = jnp.exp(own_top - best)
    carry = (
        tuple(s * own_factor[:, g:g + 1] for g, s in enumerate(own_sums)),
        own_total * own_factor)
    carry = add(res_out[0], carry)
    sums, total = fold(1, n, lambda k, c: add(res_in[k], c), carry)
    for g in range(parts):
        att_rows[g * TILE:(g + 1) * TILE, :] = sums[g] / total[:, g:g + 1]
    att[...] = jnp.concatenate(
        [att_rows[row_of(g, h):row_of(g, h) + BRANCHES, :]
         for g in range(kv_local) for h in range(GROUP)], axis=1).astype(BF16)

    def drain(k):
        q_copy(k).wait_send()
        p_copy(k).wait_send()
        r_copy(k).wait_send()

    each(1, n, drain)


def place(*refs):
    count = len(refs) // 2
    sems = refs[-1]
    copies = [
        pltpu.make_async_copy(refs[i], refs[count + i], sems.at[i]) for i in range(count)]
    for item in copies:
        item.start()
    for item in copies:
        item.wait()


def shards(n, *args):
    queries, prefix_keys, prefix_values, suffix_keys, suffix_values = args[:5]
    new_keys, new_values, suffix_lengths, fork_list = args[5:]
    slots, width = suffix_keys.shape[1:]
    kv_local = width // HD
    rows = (kv_local + 2) * TILE
    assert queries.shape[0] == BRANCHES and fork_list.shape[0] == 1
    assert n * BRANCHES <= 256 and rows % 16 == 0 and n & (n - 1) == 0
    dma = pltpu.SemaphoreType.DMA
    hbm_spec = pl.BlockSpec(memory_space=pltpu.HBM)
    vmem_spec = pl.BlockSpec(memory_space=pltpu.VMEM)
    like = lambda x: pltpu.VMEM(x.shape, x.dtype)
    out_shape = (
        jax.ShapeDtypeStruct(queries.shape, BF16),
        jax.ShapeDtypeStruct(suffix_keys.shape, BF16),
        jax.ShapeDtypeStruct(suffix_values.shape, BF16),
    )
    results = pl.pallas_call(
        functools.partial(kernel, n),
        out_shape=out_shape,
        in_specs=[hbm_spec] * 9,
        out_specs=(vmem_spec,) * 3,
        scratch_shapes=[
            like(queries), like(prefix_keys), like(prefix_values), like(suffix_keys),
            like(suffix_values), like(new_keys), like(new_values),
            pltpu.SMEM(suffix_lengths.shape, jnp.int32), pltpu.SMEM(fork_list.shape, jnp.int32),
            pltpu.VMEM((rows, HD), F32),
            pltpu.VMEM((n, rows, HD), BF16),
            pltpu.VMEM((n, 2 * slots, width), BF16),
            pltpu.VMEM((n, rows, HD), BF16),
            pltpu.VMEM((n, rows, HD), BF16),
            pltpu.VMEM((rows, HD), F32),
            dma((9,)),
        ] + [dma((n,))] * 6,
        compiler_params=pltpu.CompilerParams(
            collective_id=0, has_side_effects=True, vmem_limit_bytes=32 * 2**20),
    )(*[pltpu.with_memory_space_constraint(x, pltpu.HBM) for x in args])
    return pl.pallas_call(
        place,
        out_shape=out_shape,
        in_specs=[vmem_spec] * 3,
        out_specs=(hbm_spec,) * 3,
        scratch_shapes=[dma((3,))],
    )(*results)


def solution(mesh):
    return jax.shard_map(
        functools.partial(shards, mesh.shape["seq"]),
        mesh=mesh,
        in_specs=(
            P(("groups", "seq"), "mp"),
            P(("groups", "seq"), "mp"),
            P(("groups", "seq"), "mp"),
            P(("groups", "seq"), None, "mp"),
            P(("groups", "seq"), None, "mp"),
            P(("groups", "seq"), "mp"),
            P(("groups", "seq"), "mp"),
            P(("groups", "seq")),
            P(("groups", "seq"), None),
        ),
        out_specs=(
            P(("groups", "seq"), "mp"),
            P(("groups", "seq"), None, "mp"),
            P(("groups", "seq"), None, "mp"),
        ),
        check_vma=False,
    )
```

```python
import functools
import math

import jax
import jax.numpy as jnp
from jax import lax
from jax.experimental import pallas as pl
from jax.experimental.pallas import tpu as pltpu
from jax.sharding import PartitionSpec as P

HQ = 40
KVH = 8
HD = 128
GROUP = HQ // KVH
BRANCHES = 2
TILE = 8
MESH = pl.DeviceIdType.MESH
NT = (((1,), (1,)), ((), ()))
UNROLL_UP_TO = 16
F32 = jnp.float32
BF16 = jnp.bfloat16


def each(start, stop, body):
    if stop - start <= UNROLL_UP_TO:
        for index in range(start, stop):
            body(index)
    else:
        def step(index, carry):
            body(index)
            return carry

        lax.fori_loop(start, stop, step, 0)


def fold(start, stop, body, carry):
    if stop - start <= UNROLL_UP_TO:
        for index in range(start, stop):
            carry = body(index, carry)
        return carry
    return lax.fori_loop(start, stop, body, carry)


def kernel(
    n,
    q_hbm, pk_hbm, pv_hbm, sk_hbm, sv_hbm, nk_hbm, nv_hbm, len_hbm, fork_hbm,
    att, ck, cv,
    q_in, pk, pv, sk, sv, nk, nv, len_ref, fork_ref,
    q_f32, q_tiles, pieces, res_out, res_in, att_rows,
    in_sem, q_send, q_recv, p_send, p_recv, r_send, r_recv,
):
    me = lax.axis_index("seq")
    slots = sk.shape[1]
    kv_local = pk.shape[1] // HD
    scale = 1.0 / math.sqrt(HD)
    base = me * BRANCHES
    rest = kv_local * TILE
    notes_at = rest + TILE
    chunk = math.gcd(n, 4)

    def partner(k):
        other, bit = me, 1
        while bit < n:
            other = other + (k // bit) % 2 * bit * (1 - 2 * ((me // bit) % 2))
            bit *= 2
        return {"seq": other}

    barrier = pltpu.get_barrier_semaphore()
    each(1, n, lambda k: pl.semaphore_signal(
        barrier, inc=1, device_id=partner(k), device_id_type=MESH))

    loads = [
        pltpu.make_async_copy(src, dst, in_sem.at[i])
        for i, (src, dst) in enumerate([
            (q_hbm, q_in), (sk_hbm, sk), (sv_hbm, sv), (pk_hbm, pk),
            (pv_hbm, pv), (nk_hbm, nk), (nv_hbm, nv), (len_hbm, len_ref), (fork_hbm, fork_ref)])
    ]
    for i in (0, 7, 8, 1, 2, 3, 4, 5, 6):
        loads[i].start()

    def row_of(g, h):
        return g * TILE + h * BRANCHES if h < GROUP - 1 else rest + g * BRANCHES

    loads[7].wait()
    loads[8].wait()
    parent = fork_ref[0, 0] - base
    parent_length = jnp.where(parent == 0, len_ref[0], len_ref[1])
    q_f32[notes_at:] = jnp.zeros((TILE, HD), F32)
    q_f32[notes_at:notes_at + 1] = jnp.full((1, HD), fork_ref[0, 1].astype(F32))
    q_f32[notes_at + 1:notes_at + 2] = jnp.full((1, HD), parent_length.astype(F32))
    loads[0].wait()
    q_all = q_in[...].astype(F32)
    for g in range(kv_local):
        for h in range(GROUP):
            at = (g * GROUP + h) * HD
            q_f32[row_of(g, h):row_of(g, h) + BRANCHES, :] = q_all[:, at:at + HD]
    q_tiles[0] = q_f32[...].astype(BF16)

    pl.semaphore_wait(barrier, n - 1)

    def copy(src, dst, send, recv, k):
        return pltpu.make_async_remote_copy(
            src_ref=src, dst_ref=dst, send_sem=send.at[k], recv_sem=recv.at[k],
            device_id=partner(k), device_id_type=MESH)

    def q_copy(k):
        return copy(q_tiles.at[0], q_tiles.at[k], q_send, q_recv, k)

    def p_copy(k):
        return copy(pieces.at[0], pieces.at[k], p_send, p_recv, k)

    def p_pass(k):
        return pltpu.make_async_remote_copy(
            src_ref=pieces.at[k], dst_ref=pieces.at[k + 1],
            send_sem=p_send.at[k + 1], recv_sem=p_recv.at[k + 1],
            device_id=partner(1), device_id_type=MESH)

    def r_copy(k):
        return copy(res_out.at[k], res_in.at[k], r_send, r_recv, k)

    def far_first(body):
        each(chunk, n, body)
        each(1, chunk, body)

    far_first(lambda k: q_copy(k).start())

    loads[1].wait()
    loads[2].wait()

    def own_suffix(j):
        return jnp.concatenate([sk[j].astype(F32), sv[j].astype(F32)], axis=0)

    parent_b = jnp.full((2 * slots, sk.shape[2]), parent.astype(F32))
    pieces[0] = jnp.where(parent_b == 0.0, own_suffix(0), own_suffix(1)).astype(BF16)
    each(1, n // 2, lambda i: p_copy(n - 2 * i).start())
    p_copy(1).start()

    loads[3].wait()
    loads[4].wait()

    count = chunk * TILE
    lane = lax.rem(lax.broadcasted_iota(jnp.int32, (count, HD), 1), 16)
    owner_s = lax.rem(lax.broadcasted_iota(jnp.int32, (count, pk.shape[0]), 0), TILE) // BRANCHES
    owner_o = lax.rem(lax.broadcasted_iota(jnp.int32, (count, HD), 0), TILE) // BRANCHES

    def softmax(scores):
        row_max = jnp.max(scores, axis=1, keepdims=True)
        weights = jnp.exp(scores - row_max)
        return row_max, jnp.sum(weights, axis=1, keepdims=True), weights.astype(BF16)

    def block(first):
        tiles = q_tiles[pl.ds(first, chunk)].astype(F32)

        def rows(at):
            return tiles[:, at:at + TILE].reshape(count, HD)

        last = rows(rest)
        scores, rest_scores = [], None
        for g in range(kv_local):
            q = jnp.concatenate([rows(g * TILE), last], axis=0).astype(BF16)
            s = lax.dot_general(
                q, pk[:, g * HD:(g + 1) * HD], NT, preferred_element_type=F32) * scale
            scores.append(s[:count])
            rest_scores = s[count:] if g == 0 else jnp.where(owner_s == g, s[count:], rest_scores)
        outputs = []
        top = jnp.zeros((count, HD), F32)
        total = jnp.ones((count, HD), F32)
        for g, s in enumerate(scores + [rest_scores]):
            row_max, row_total, weights = softmax(s)
            if g < kv_local:
                summed = jnp.dot(
                    weights, pv[:, g * HD:(g + 1) * HD], preferred_element_type=F32)
            else:
                every = jnp.dot(weights, pv[...], preferred_element_type=F32)
                summed = every[:, :HD]
                for i in range(1, kv_local):
                    summed = jnp.where(owner_o == i, every[:, i * HD:(i + 1) * HD], summed)
            outputs.append(summed * (1.0 / row_total))
            top = jnp.where(lane == g, row_max, top)
            total = jnp.where(lane == g, row_total, total)
        lse = top + jnp.log(total)
        high = lse.astype(BF16).astype(F32)
        middle = (lse - high).astype(BF16).astype(F32)
        low = lse - high - middle
        at = lax.broadcasted_iota(jnp.int32, (count, HD), 1) // 16
        outputs.append(jnp.where(at == 0, high, jnp.where(at == 1, middle, low)))
        res_out[pl.ds(first, chunk)] = jnp.concatenate(
            [o.reshape(chunk, TILE, HD) for o in outputs], axis=1).astype(BF16)

    each(1, chunk, lambda k: q_copy(k).wait_recv())
    block(0)
    each(1, chunk, lambda k: r_copy(k).start())

    def far_block(index):
        first = index * chunk
        each(0, chunk, lambda i: q_copy(first + i).wait_recv())
        block(first)
        each(0, chunk, lambda i: r_copy(first + i).start())

    each(1, n // chunk, far_block)

    def pass_on(i):
        p_copy(2 * i).wait_recv()
        p_pass(2 * i).start()

    each(1, n // 2, pass_on)
    p_copy(1).wait_recv()
    each(1, n // 2, lambda i: p_pass(2 * i).wait_recv())
    loads[5].wait()
    loads[6].wait()
    blocks = sk.shape[2] // HD

    def wide(row):
        return jnp.concatenate([jnp.broadcast_to(row, (2 * slots, HD))] * blocks, axis=1)

    def land(k, carry):
        notes = q_tiles[k].astype(F32)[notes_at:]
        child, child_length = wide(notes[:1]), wide(notes[1:2])
        arrived = pieces[k].astype(F32)
        out = []
        for j in range(BRANCHES):
            cache, length = carry[j]
            mine = child == (base + j).astype(F32)
            out.append((jnp.where(mine, arrived, cache), jnp.where(mine, child_length, length)))
        return tuple(out)

    shape = (2 * slots, sk.shape[2])
    landed = fold(0, n, land, tuple(
        (own_suffix(j), jnp.full(shape, len_ref[j].astype(F32))) for j in range(BRANCHES)))

    slot = lax.rem(lax.broadcasted_iota(jnp.int32, shape, 0), slots).astype(F32)
    nk_all, nv_all = nk[...].astype(F32), nv[...].astype(F32)
    caches = []
    for j in range(BRANCHES):
        cache, length = landed[j]
        fresh = jnp.concatenate([
            jnp.broadcast_to(nk_all[j:j + 1], (slots, shape[1])),
            jnp.broadcast_to(nv_all[j:j + 1], (slots, shape[1]))], axis=0)
        cache = jnp.where(slot == length, fresh, cache)
        ck[j] = cache[:slots].astype(BF16)
        cv[j] = cache[slots:].astype(BF16)
        caches.append(cache)

    parts = kv_local + 1
    keys_count = BRANCHES * slots
    row_id = lax.broadcasted_iota(jnp.int32, (parts * TILE, keys_count), 0)
    key_id = lax.broadcasted_iota(jnp.int32, (parts * TILE, keys_count), 1)
    key_length = jnp.where(
        key_id[:1] >= slots, landed[1][1][:1, :keys_count], landed[0][1][:1, :keys_count])
    live = jnp.logical_and(
        lax.rem(row_id, BRANCHES) == key_id // slots,
        lax.rem(key_id, slots).astype(F32) <= jnp.broadcast_to(key_length, row_id.shape))
    own_q = q_f32[...]
    own_scores, rest_scores = [], None
    owner = lax.broadcasted_iota(jnp.int32, (TILE, HD), 0) // BRANCHES
    for g in range(kv_local):
        keys = jnp.concatenate(
            [c[:slots, g * HD:(g + 1) * HD] for c in caches], axis=0).astype(BF16)
        q = jnp.concatenate(
            [own_q[g * TILE:(g + 1) * TILE], own_q[rest:notes_at]], axis=0).astype(BF16)
        s = lax.dot_general(q, keys, NT, preferred_element_type=F32) * scale
        own_scores.append(s[:TILE])
        rest_scores = s[TILE:] if g == 0 else jnp.where(
            owner[:, :keys_count] == g, s[TILE:], rest_scores)
    scores = jnp.concatenate(own_scores + [rest_scores], axis=0)
    row_max = jnp.max(jnp.where(live, scores, -jnp.inf), axis=1, keepdims=True)
    weights = jnp.where(live, jnp.exp(scores - row_max), 0.0)
    row_total = jnp.sum(weights, axis=1, keepdims=True)
    own_sums, rest_sum = [], None
    for g in range(kv_local):
        values = jnp.concatenate(
            [c[slots:, g * HD:(g + 1) * HD] for c in caches], axis=0).astype(BF16)
        w = jnp.concatenate(
            [weights[g * TILE:(g + 1) * TILE], weights[rest:notes_at]], axis=0).astype(BF16)
        o = jnp.dot(w, values, preferred_element_type=F32)
        own_sums.append(o[:TILE])
        rest_sum = o[TILE:] if g == 0 else jnp.where(owner == g, o[TILE:], rest_sum)
    own_sums.append(rest_sum)
    lane = lax.broadcasted_iota(jnp.int32, (TILE, HD), 1)
    own_top = jnp.zeros((TILE, HD), F32)
    own_total = jnp.ones((TILE, HD), F32)
    for g in range(parts):
        at = slice(g * TILE, (g + 1) * TILE)
        own_top = jnp.where(lane == g, row_max[at], own_top)
        own_total = jnp.where(lane == g, row_total[at], own_total)

    def lse_of(tile):
        terms = tile.astype(F32)[notes_at:]
        return terms + pltpu.roll(terms, HD - 16, 1) + pltpu.roll(terms, HD - 32, 1)

    each(1, n, lambda k: r_copy(k).wait_recv())
    best = fold(
        1, n, lambda k, m: jnp.maximum(m, lse_of(res_in[k])),
        jnp.maximum(own_top, lse_of(res_out[0])))

    def add(tile, carry):
        sums, total = carry
        factor = jnp.exp(lse_of(tile) - best)
        tile = tile.astype(F32)
        sums = tuple(
            s + tile[g * TILE:(g + 1) * TILE] * factor[:, g:g + 1] for g, s in enumerate(sums))
        return sums, total + factor

    own_factor = jnp.exp(own_top - best)
    carry = (
        tuple(s * own_factor[:, g:g + 1] for g, s in enumerate(own_sums)),
        own_total * own_factor)
    carry = add(res_out[0], carry)
    sums, total = fold(1, n, lambda k, c: add(res_in[k], c), carry)
    for g in range(parts):
        att_rows[g * TILE:(g + 1) * TILE, :] = sums[g] / total[:, g:g + 1]
    att[...] = jnp.concatenate(
        [att_rows[row_of(g, h):row_of(g, h) + BRANCHES, :]
         for g in range(kv_local) for h in range(GROUP)], axis=1).astype(BF16)

    def drain(k):
        q_copy(k).wait_send()
        r_copy(k).wait_send()

    def drain_pieces(i):
        p_copy(2 * i).wait_send()
        p_pass(2 * i).wait_send()

    each(1, n, drain)
    p_copy(1).wait_send()
    each(1, n // 2, drain_pieces)


def place(*refs):
    count = len(refs) // 2
    sems = refs[-1]
    copies = [
        pltpu.make_async_copy(refs[i], refs[count + i], sems.at[i]) for i in range(count)]
    for item in copies:
        item.start()
    for item in copies:
        item.wait()


def shards(n, *args):
    queries, prefix_keys, prefix_values, suffix_keys, suffix_values = args[:5]
    new_keys, new_values, suffix_lengths, fork_list = args[5:]
    slots, width = suffix_keys.shape[1:]
    kv_local = width // HD
    rows = (kv_local + 2) * TILE
    assert queries.shape[0] == BRANCHES and fork_list.shape[0] == 1
    assert n * BRANCHES <= 256 and rows % 16 == 0 and n & (n - 1) == 0
    dma = pltpu.SemaphoreType.DMA
    hbm_spec = pl.BlockSpec(memory_space=pltpu.HBM)
    vmem_spec = pl.BlockSpec(memory_space=pltpu.VMEM)
    like = lambda x: pltpu.VMEM(x.shape, x.dtype)
    out_shape = (
        jax.ShapeDtypeStruct(queries.shape, BF16),
        jax.ShapeDtypeStruct(suffix_keys.shape, BF16),
        jax.ShapeDtypeStruct(suffix_values.shape, BF16),
    )
    results = pl.pallas_call(
        functools.partial(kernel, n),
        out_shape=out_shape,
        in_specs=[hbm_spec] * 9,
        out_specs=(vmem_spec,) * 3,
        scratch_shapes=[
            like(queries), like(prefix_keys), like(prefix_values), like(suffix_keys),
            like(suffix_values), like(new_keys), like(new_values),
            pltpu.SMEM(suffix_lengths.shape, jnp.int32), pltpu.SMEM(fork_list.shape, jnp.int32),
            pltpu.VMEM((rows, HD), F32),
            pltpu.VMEM((n, rows, HD), BF16),
            pltpu.VMEM((n, 2 * slots, width), BF16),
            pltpu.VMEM((n, rows, HD), BF16),
            pltpu.VMEM((n, rows, HD), BF16),
            pltpu.VMEM((rows, HD), F32),
            dma((9,)),
        ] + [dma((n,))] * 6,
        compiler_params=pltpu.CompilerParams(
            collective_id=0, has_side_effects=True, vmem_limit_bytes=32 * 2**20),
    )(*[pltpu.with_memory_space_constraint(x, pltpu.HBM) for x in args])
    return pl.pallas_call(
        place,
        out_shape=out_shape,
        in_specs=[vmem_spec] * 3,
        out_specs=(hbm_spec,) * 3,
        scratch_shapes=[dma((3,))],
        compiler_params=pltpu.CompilerParams(vmem_limit_bytes=2**20),
    )(*results)


def solution(mesh):
    return jax.shard_map(
        functools.partial(shards, mesh.shape["seq"]),
        mesh=mesh,
        in_specs=(
            P(("groups", "seq"), "mp"),
            P(("groups", "seq"), "mp"),
            P(("groups", "seq"), "mp"),
            P(("groups", "seq"), None, "mp"),
            P(("groups", "seq"), None, "mp"),
            P(("groups", "seq"), "mp"),
            P(("groups", "seq"), "mp"),
            P(("groups", "seq")),
            P(("groups", "seq"), None),
        ),
        out_specs=(
            P(("groups", "seq"), "mp"),
            P(("groups", "seq"), None, "mp"),
            P(("groups", "seq"), None, "mp"),
        ),
        check_vma=False,
    )
```

```python
import functools
import math

import jax
import jax.numpy as jnp
from jax import lax
from jax.experimental import pallas as pl
from jax.experimental.pallas import tpu as pltpu
from jax.sharding import PartitionSpec as P

HQ = 40
KVH = 8
HD = 128
GROUP = HQ // KVH
BRANCHES = 2
TILE = 8
MESH = pl.DeviceIdType.MESH
NT = (((1,), (1,)), ((), ()))
UNROLL_UP_TO = 16
F32 = jnp.float32
BF16 = jnp.bfloat16


def each(start, stop, body):
    if stop - start <= UNROLL_UP_TO:
        for index in range(start, stop):
            body(index)
    else:
        def step(index, carry):
            body(index)
            return carry

        lax.fori_loop(start, stop, step, 0)


def fold(start, stop, body, carry):
    if stop - start <= UNROLL_UP_TO:
        for index in range(start, stop):
            carry = body(index, carry)
        return carry
    return lax.fori_loop(start, stop, body, carry)


def kernel(
    n,
    q_hbm, pk_hbm, pv_hbm, sk_hbm, sv_hbm, nk_hbm, nv_hbm, len_hbm, fork_hbm,
    att, ck, cv,
    q_in, pk, pv, sk, sv, nk, nv, len_ref, fork_ref,
    q_f32, q_tiles, pieces, res_out, res_in, att_rows,
    in_sem, q_send, q_recv, p_send, p_recv, r_send, r_recv,
):
    me = lax.axis_index("seq")
    slots = sk.shape[1]
    kv_local = pk.shape[1] // HD
    scale = 1.0 / math.sqrt(HD)
    base = me * BRANCHES
    rest = kv_local * TILE
    notes_at = rest + TILE
    chunk = math.gcd(n, 4)

    def partner(k):
        other, bit = me, 1
        while bit < n:
            other = other + (k // bit) % 2 * bit * (1 - 2 * ((me // bit) % 2))
            bit *= 2
        return {"seq": other}

    barrier = pltpu.get_barrier_semaphore()
    each(1, n, lambda k: pl.semaphore_signal(
        barrier, inc=1, device_id=partner(k), device_id_type=MESH))

    loads = [
        pltpu.make_async_copy(src, dst, in_sem.at[i])
        for i, (src, dst) in enumerate([
            (q_hbm, q_in), (sk_hbm, sk), (sv_hbm, sv), (pk_hbm, pk),
            (pv_hbm, pv), (nk_hbm, nk), (nv_hbm, nv), (len_hbm, len_ref), (fork_hbm, fork_ref)])
    ]
    for i in (0, 7, 8, 1, 2, 3, 4, 5, 6):
        loads[i].start()

    def row_of(g, h):
        return g * TILE + h * BRANCHES if h < GROUP - 1 else rest + g * BRANCHES

    loads[7].wait()
    loads[8].wait()
    parent = fork_ref[0, 0] - base
    parent_length = jnp.where(parent == 0, len_ref[0], len_ref[1])
    q_f32[notes_at:] = jnp.zeros((TILE, HD), F32)
    q_f32[notes_at:notes_at + 1] = jnp.full((1, HD), fork_ref[0, 1].astype(F32))
    q_f32[notes_at + 1:notes_at + 2] = jnp.full((1, HD), parent_length.astype(F32))
    loads[0].wait()
    q_all = q_in[...].astype(F32)
    for g in range(kv_local):
        for h in range(GROUP):
            at = (g * GROUP + h) * HD
            q_f32[row_of(g, h):row_of(g, h) + BRANCHES, :] = q_all[:, at:at + HD]
    q_tiles[0] = q_f32[...].astype(BF16)

    loads[1].wait()
    loads[2].wait()

    def own_suffix(j):
        return jnp.concatenate([sk[j].astype(F32), sv[j].astype(F32)], axis=0)

    parent_b = jnp.full((2 * slots, sk.shape[2]), parent.astype(F32))
    pieces[0] = jnp.where(parent_b == 0.0, own_suffix(0), own_suffix(1)).astype(BF16)

    pl.semaphore_wait(barrier, n - 1)

    def copy(src, dst, send, recv, k):
        return pltpu.make_async_remote_copy(
            src_ref=src, dst_ref=dst, send_sem=send.at[k], recv_sem=recv.at[k],
            device_id=partner(k), device_id_type=MESH)

    def q_copy(k):
        return copy(q_tiles.at[0], q_tiles.at[k], q_send, q_recv, k)

    def p_copy(k):
        return copy(pieces.at[0], pieces.at[k], p_send, p_recv, k)

    def p_pass(k):
        return pltpu.make_async_remote_copy(
            src_ref=pieces.at[k], dst_ref=pieces.at[k + 1],
            send_sem=p_send.at[k + 1], recv_sem=p_recv.at[k + 1],
            device_id=partner(1), device_id_type=MESH)

    def r_copy(k):
        return copy(res_out.at[k], res_in.at[k], r_send, r_recv, k)

    def far_first(body):
        each(chunk, n, body)
        each(1, chunk, body)

    each(1, n // 2, lambda i: p_copy(n - 2 * i).start())
    far_first(lambda k: q_copy(k).start())
    p_copy(1).start()

    loads[3].wait()
    loads[4].wait()

    count = chunk * TILE
    lane = lax.rem(lax.broadcasted_iota(jnp.int32, (count, HD), 1), 16)
    owner_s = lax.rem(lax.broadcasted_iota(jnp.int32, (count, pk.shape[0]), 0), TILE) // BRANCHES
    owner_o = lax.rem(lax.broadcasted_iota(jnp.int32, (count, HD), 0), TILE) // BRANCHES

    def softmax(scores):
        row_max = jnp.max(scores, axis=1, keepdims=True)
        weights = jnp.exp(scores - row_max)
        return row_max, jnp.sum(weights, axis=1, keepdims=True), weights.astype(BF16)

    def block(first):
        tiles = q_tiles[pl.ds(first, chunk)].astype(F32)

        def rows(at):
            return tiles[:, at:at + TILE].reshape(count, HD)

        last = rows(rest)
        scores, rest_scores = [], None
        for g in range(kv_local):
            q = jnp.concatenate([rows(g * TILE), last], axis=0).astype(BF16)
            s = lax.dot_general(
                q, pk[:, g * HD:(g + 1) * HD], NT, preferred_element_type=F32) * scale
            scores.append(s[:count])
            rest_scores = s[count:] if g == 0 else jnp.where(owner_s == g, s[count:], rest_scores)
        outputs = []
        top = jnp.zeros((count, HD), F32)
        total = jnp.ones((count, HD), F32)
        for g, s in enumerate(scores + [rest_scores]):
            row_max, row_total, weights = softmax(s)
            if g < kv_local:
                summed = jnp.dot(
                    weights, pv[:, g * HD:(g + 1) * HD], preferred_element_type=F32)
            else:
                every = jnp.dot(weights, pv[...], preferred_element_type=F32)
                summed = every[:, :HD]
                for i in range(1, kv_local):
                    summed = jnp.where(owner_o == i, every[:, i * HD:(i + 1) * HD], summed)
            outputs.append(summed * (1.0 / row_total))
            top = jnp.where(lane == g, row_max, top)
            total = jnp.where(lane == g, row_total, total)
        lse = top + jnp.log(total)
        high = lse.astype(BF16).astype(F32)
        middle = (lse - high).astype(BF16).astype(F32)
        low = lse - high - middle
        at = lax.broadcasted_iota(jnp.int32, (count, HD), 1) // 16
        outputs.append(jnp.where(at == 0, high, jnp.where(at == 1, middle, low)))
        res_out[pl.ds(first, chunk)] = jnp.concatenate(
            [o.reshape(chunk, TILE, HD) for o in outputs], axis=1).astype(BF16)

    def pass_on(i):
        p_copy(2 * i).wait_recv()
        p_pass(2 * i).start()

    each(1, n // 2, pass_on)
    each(1, chunk, lambda k: q_copy(k).wait_recv())
    block(0)
    each(1, chunk, lambda k: r_copy(k).start())

    def far_block(index):
        first = index * chunk
        each(0, chunk, lambda i: q_copy(first + i).wait_recv())
        block(first)
        each(0, chunk, lambda i: r_copy(first + i).start())

    each(1, n // chunk, far_block)

    loads[5].wait()
    loads[6].wait()
    blocks = sk.shape[2] // HD

    def wide(row):
        return jnp.concatenate([jnp.broadcast_to(row, (2 * slots, HD))] * blocks, axis=1)

    def land(k, carry):
        notes = q_tiles[k].astype(F32)[notes_at:]
        child, child_length = wide(notes[:1]), wide(notes[1:2])
        arrived = pieces[k].astype(F32)
        out = []
        for j in range(BRANCHES):
            cache, length = carry[j]
            mine = child == (base + j).astype(F32)
            out.append((jnp.where(mine, arrived, cache), jnp.where(mine, child_length, length)))
        return tuple(out)

    shape = (2 * slots, sk.shape[2])
    landed = tuple(
        (own_suffix(j), jnp.full(shape, len_ref[j].astype(F32))) for j in range(BRANCHES))
    landed = fold(0, n // 2, lambda i, c: land(2 * i, c), landed)
    p_copy(1).wait_recv()
    each(1, n // 2, lambda i: p_pass(2 * i).wait_recv())
    landed = fold(0, n // 2, lambda i, c: land(2 * i + 1, c), landed)

    slot = lax.rem(lax.broadcasted_iota(jnp.int32, shape, 0), slots).astype(F32)
    nk_all, nv_all = nk[...].astype(F32), nv[...].astype(F32)
    caches = []
    for j in range(BRANCHES):
        cache, length = landed[j]
        fresh = jnp.concatenate([
            jnp.broadcast_to(nk_all[j:j + 1], (slots, shape[1])),
            jnp.broadcast_to(nv_all[j:j + 1], (slots, shape[1]))], axis=0)
        cache = jnp.where(slot == length, fresh, cache)
        ck[j] = cache[:slots].astype(BF16)
        cv[j] = cache[slots:].astype(BF16)
        caches.append(cache)

    parts = kv_local + 1
    keys_count = BRANCHES * slots
    row_id = lax.broadcasted_iota(jnp.int32, (parts * TILE, keys_count), 0)
    key_id = lax.broadcasted_iota(jnp.int32, (parts * TILE, keys_count), 1)
    key_length = jnp.where(
        key_id[:1] >= slots, landed[1][1][:1, :keys_count], landed[0][1][:1, :keys_count])
    live = jnp.logical_and(
        lax.rem(row_id, BRANCHES) == key_id // slots,
        lax.rem(key_id, slots).astype(F32) <= jnp.broadcast_to(key_length, row_id.shape))
    own_q = q_f32[...]
    own_scores, rest_scores = [], None
    owner = lax.broadcasted_iota(jnp.int32, (TILE, HD), 0) // BRANCHES
    for g in range(kv_local):
        keys = jnp.concatenate(
            [c[:slots, g * HD:(g + 1) * HD] for c in caches], axis=0).astype(BF16)
        q = jnp.concatenate(
            [own_q[g * TILE:(g + 1) * TILE], own_q[rest:notes_at]], axis=0).astype(BF16)
        s = lax.dot_general(q, keys, NT, preferred_element_type=F32) * scale
        own_scores.append(s[:TILE])
        rest_scores = s[TILE:] if g == 0 else jnp.where(
            owner[:, :keys_count] == g, s[TILE:], rest_scores)
    scores = jnp.concatenate(own_scores + [rest_scores], axis=0)
    row_max = jnp.max(jnp.where(live, scores, -jnp.inf), axis=1, keepdims=True)
    weights = jnp.where(live, jnp.exp(scores - row_max), 0.0)
    row_total = jnp.sum(weights, axis=1, keepdims=True)
    own_sums, rest_sum = [], None
    for g in range(kv_local):
        values = jnp.concatenate(
            [c[slots:, g * HD:(g + 1) * HD] for c in caches], axis=0).astype(BF16)
        w = jnp.concatenate(
            [weights[g * TILE:(g + 1) * TILE], weights[rest:notes_at]], axis=0).astype(BF16)
        o = jnp.dot(w, values, preferred_element_type=F32)
        own_sums.append(o[:TILE])
        rest_sum = o[TILE:] if g == 0 else jnp.where(owner == g, o[TILE:], rest_sum)
    own_sums.append(rest_sum)
    lane = lax.broadcasted_iota(jnp.int32, (TILE, HD), 1)
    own_top = jnp.zeros((TILE, HD), F32)
    own_total = jnp.ones((TILE, HD), F32)
    for g in range(parts):
        at = slice(g * TILE, (g + 1) * TILE)
        own_top = jnp.where(lane == g, row_max[at], own_top)
        own_total = jnp.where(lane == g, row_total[at], own_total)

    def lse_of(tile):
        terms = tile.astype(F32)[notes_at:]
        return terms + pltpu.roll(terms, HD - 16, 1) + pltpu.roll(terms, HD - 32, 1)

    def highest(k, m):
        return jnp.maximum(m, lse_of(res_in[k]))

    def add(tile, best, carry):
        sums, total = carry
        factor = jnp.exp(lse_of(tile) - best)
        tile = tile.astype(F32)
        sums = tuple(
            s + tile[g * TILE:(g + 1) * TILE] * factor[:, g:g + 1] for g, s in enumerate(sums))
        return sums, total + factor

    def scaled(factor, sums, total):
        return tuple(s * factor[:, g:g + 1] for g, s in enumerate(sums)), total * factor

    each(1, chunk, lambda k: r_copy(k).wait_recv())
    near = fold(1, chunk, highest, jnp.maximum(own_top, lse_of(res_out[0])))
    carry = scaled(jnp.exp(own_top - near), own_sums, own_total)
    carry = add(res_out[0], near, carry)
    carry = fold(1, chunk, lambda k, c: add(res_in[k], near, c), carry)
    each(chunk, n, lambda k: r_copy(k).wait_recv())
    best = fold(chunk, n, highest, near)
    carry = scaled(jnp.exp(near - best), *carry)
    sums, total = fold(chunk, n, lambda k, c: add(res_in[k], best, c), carry)
    for g in range(parts):
        att_rows[g * TILE:(g + 1) * TILE, :] = sums[g] / total[:, g:g + 1]
    att[...] = jnp.concatenate(
        [att_rows[row_of(g, h):row_of(g, h) + BRANCHES, :]
         for g in range(kv_local) for h in range(GROUP)], axis=1).astype(BF16)

    def drain(k):
        q_copy(k).wait_send()
        r_copy(k).wait_send()

    def drain_pieces(i):
        p_copy(2 * i).wait_send()
        p_pass(2 * i).wait_send()

    each(1, n, drain)
    p_copy(1).wait_send()
    each(1, n // 2, drain_pieces)


def place(*refs):
    count = len(refs) // 2
    sems = refs[-1]
    copies = [
        pltpu.make_async_copy(refs[i], refs[count + i], sems.at[i]) for i in range(count)]
    for item in copies:
        item.start()
    for item in copies:
        item.wait()


def shards(n, *args):
    queries, prefix_keys, prefix_values, suffix_keys, suffix_values = args[:5]
    new_keys, new_values, suffix_lengths, fork_list = args[5:]
    slots, width = suffix_keys.shape[1:]
    kv_local = width // HD
    rows = (kv_local + 2) * TILE
    assert queries.shape[0] == BRANCHES and fork_list.shape[0] == 1
    assert n * BRANCHES <= 256 and rows % 16 == 0 and n & (n - 1) == 0
    dma = pltpu.SemaphoreType.DMA
    hbm_spec = pl.BlockSpec(memory_space=pltpu.HBM)
    vmem_spec = pl.BlockSpec(memory_space=pltpu.VMEM)
    like = lambda x: pltpu.VMEM(x.shape, x.dtype)
    out_shape = (
        jax.ShapeDtypeStruct(queries.shape, BF16),
        jax.ShapeDtypeStruct(suffix_keys.shape, BF16),
        jax.ShapeDtypeStruct(suffix_values.shape, BF16),
    )
    results = pl.pallas_call(
        functools.partial(kernel, n),
        out_shape=out_shape,
        in_specs=[hbm_spec] * 9,
        out_specs=(vmem_spec,) * 3,
        scratch_shapes=[
            like(queries), like(prefix_keys), like(prefix_values), like(suffix_keys),
            like(suffix_values), like(new_keys), like(new_values),
            pltpu.SMEM(suffix_lengths.shape, jnp.int32), pltpu.SMEM(fork_list.shape, jnp.int32),
            pltpu.VMEM((rows, HD), F32),
            pltpu.VMEM((n, rows, HD), BF16),
            pltpu.VMEM((n, 2 * slots, width), BF16),
            pltpu.VMEM((n, rows, HD), BF16),
            pltpu.VMEM((n, rows, HD), BF16),
            pltpu.VMEM((rows, HD), F32),
            dma((9,)),
        ] + [dma((n,))] * 6,
        compiler_params=pltpu.CompilerParams(
            collective_id=0, has_side_effects=True, vmem_limit_bytes=32 * 2**20),
    )(*[pltpu.with_memory_space_constraint(x, pltpu.HBM) for x in args])
    return pl.pallas_call(
        place,
        out_shape=out_shape,
        in_specs=[vmem_spec] * 3,
        out_specs=(hbm_spec,) * 3,
        scratch_shapes=[dma((3,))],
        compiler_params=pltpu.CompilerParams(vmem_limit_bytes=2**20),
    )(*results)


def solution(mesh):
    return jax.shard_map(
        functools.partial(shards, mesh.shape["seq"]),
        mesh=mesh,
        in_specs=(
            P(("groups", "seq"), "mp"),
            P(("groups", "seq"), "mp"),
            P(("groups", "seq"), "mp"),
            P(("groups", "seq"), None, "mp"),
            P(("groups", "seq"), None, "mp"),
            P(("groups", "seq"), "mp"),
            P(("groups", "seq"), "mp"),
            P(("groups", "seq")),
            P(("groups", "seq"), None),
        ),
        out_specs=(
            P(("groups", "seq"), "mp"),
            P(("groups", "seq"), None, "mp"),
            P(("groups", "seq"), None, "mp"),
        ),
        check_vma=False,
    )
```

```python
import functools
import math

import jax
import jax.numpy as jnp
from jax import lax
from jax.experimental import pallas as pl
from jax.experimental.pallas import tpu as pltpu
from jax.sharding import PartitionSpec as P

HQ = 40
KVH = 8
HD = 128
GROUP = HQ // KVH
BRANCHES = 2
TILE = 8
MESH = pl.DeviceIdType.MESH
NT = (((1,), (1,)), ((), ()))
UNROLL_UP_TO = 16
F32 = jnp.float32
BF16 = jnp.bfloat16


def each(start, stop, body):
    if stop - start <= UNROLL_UP_TO:
        for index in range(start, stop):
            body(index)
    else:
        def step(index, carry):
            body(index)
            return carry

        lax.fori_loop(start, stop, step, 0)


def fold(start, stop, body, carry):
    if stop - start <= UNROLL_UP_TO:
        for index in range(start, stop):
            carry = body(index, carry)
        return carry
    return lax.fori_loop(start, stop, body, carry)


def kernel(
    n,
    q_hbm, pk_hbm, pv_hbm, sk_hbm, sv_hbm, nk_hbm, nv_hbm, len_hbm, fork_hbm,
    att, ck, cv,
    q_in, pk, pv, sk, sv, nk, nv, len_ref, fork_ref,
    q_f32, q_tiles, pieces, res_out, res_in, att_rows,
    in_sem, q_send, q_recv, p_send, p_recv, r_send, r_recv,
):
    me = lax.axis_index("seq")
    slots = sk.shape[1]
    kv_local = pk.shape[1] // HD
    scale = 1.0 / math.sqrt(HD)
    base = me * BRANCHES
    rest = kv_local * TILE
    notes_at = rest + TILE
    chunk = math.gcd(n, 4)

    def partner(k):
        other, bit = me, 1
        while bit < n:
            other = other + (k // bit) % 2 * bit * (1 - 2 * ((me // bit) % 2))
            bit *= 2
        return {"seq": other}

    barrier = pltpu.get_barrier_semaphore()
    each(1, n, lambda k: pl.semaphore_signal(
        barrier, inc=1, device_id=partner(k), device_id_type=MESH))

    loads = [
        pltpu.make_async_copy(src, dst, in_sem.at[i])
        for i, (src, dst) in enumerate([
            (q_hbm, q_in), (sk_hbm, sk), (sv_hbm, sv), (pk_hbm, pk),
            (pv_hbm, pv), (nk_hbm, nk), (nv_hbm, nv), (len_hbm, len_ref), (fork_hbm, fork_ref)])
    ]
    for i in (0, 7, 8, 1, 2, 3, 4, 5, 6):
        loads[i].start()

    def row_of(g, h):
        return g * TILE + h * BRANCHES if h < GROUP - 1 else rest + g * BRANCHES

    loads[7].wait()
    loads[8].wait()
    parent = fork_ref[0, 0] - base
    parent_length = jnp.where(parent == 0, len_ref[0], len_ref[1])
    q_f32[notes_at:] = jnp.zeros((TILE, HD), F32)
    q_f32[notes_at:notes_at + 1] = jnp.full((1, HD), fork_ref[0, 1].astype(F32))
    q_f32[notes_at + 1:notes_at + 2] = jnp.full((1, HD), parent_length.astype(F32))
    loads[0].wait()
    q_all = q_in[...].astype(F32)
    for g in range(kv_local):
        for h in range(GROUP):
            at = (g * GROUP + h) * HD
            q_f32[row_of(g, h):row_of(g, h) + BRANCHES, :] = q_all[:, at:at + HD]
    q_tiles[0] = q_f32[...].astype(BF16)

    loads[1].wait()
    loads[2].wait()

    def own_suffix(j):
        return jnp.concatenate([sk[j].astype(F32), sv[j].astype(F32)], axis=0)

    parent_b = jnp.full((2 * slots, sk.shape[2]), parent.astype(F32))
    pieces[0] = jnp.where(parent_b == 0.0, own_suffix(0), own_suffix(1)).astype(BF16)

    pl.semaphore_wait(barrier, n - 1)

    def copy(src, dst, send, recv, k):
        return pltpu.make_async_remote_copy(
            src_ref=src, dst_ref=dst, send_sem=send.at[k], recv_sem=recv.at[k],
            device_id=partner(k), device_id_type=MESH)

    def q_copy(k):
        return copy(q_tiles.at[0], q_tiles.at[k], q_send, q_recv, k)

    def p_copy(k):
        return copy(pieces.at[0], pieces.at[k], p_send, p_recv, k)

    def p_pass(k):
        return pltpu.make_async_remote_copy(
            src_ref=pieces.at[k], dst_ref=pieces.at[k + 1],
            send_sem=p_send.at[k + 1], recv_sem=p_recv.at[k + 1],
            device_id=partner(1), device_id_type=MESH)

    def r_copy(k):
        return copy(res_out.at[k], res_in.at[k], r_send, r_recv, k)

    def far_first(body):
        each(chunk, n, body)
        each(1, chunk, body)

    far_first(lambda k: q_copy(k).start())
    each(1, n // 2, lambda i: p_copy(n - 2 * i).start())
    p_copy(1).start()

    loads[3].wait()
    loads[4].wait()

    count = chunk * TILE
    lane = lax.rem(lax.broadcasted_iota(jnp.int32, (count, HD), 1), 16)
    owner_s = lax.rem(lax.broadcasted_iota(jnp.int32, (count, pk.shape[0]), 0), TILE) // BRANCHES
    owner_o = lax.rem(lax.broadcasted_iota(jnp.int32, (count, HD), 0), TILE) // BRANCHES

    def softmax(scores):
        row_max = jnp.max(scores, axis=1, keepdims=True)
        weights = jnp.exp(scores - row_max)
        return row_max, jnp.sum(weights, axis=1, keepdims=True), weights.astype(BF16)

    def block(first):
        tiles = q_tiles[pl.ds(first, chunk)].astype(F32)

        def rows(at):
            return tiles[:, at:at + TILE].reshape(count, HD)

        last = rows(rest)
        scores, rest_scores = [], None
        for g in range(kv_local):
            q = jnp.concatenate([rows(g * TILE), last], axis=0).astype(BF16)
            s = lax.dot_general(
                q, pk[:, g * HD:(g + 1) * HD], NT, preferred_element_type=F32) * scale
            scores.append(s[:count])
            rest_scores = s[count:] if g == 0 else jnp.where(owner_s == g, s[count:], rest_scores)
        outputs = []
        top = jnp.zeros((count, HD), F32)
        total = jnp.ones((count, HD), F32)
        for g, s in enumerate(scores + [rest_scores]):
            row_max, row_total, weights = softmax(s)
            if g < kv_local:
                summed = jnp.dot(
                    weights, pv[:, g * HD:(g + 1) * HD], preferred_element_type=F32)
            else:
                every = jnp.dot(weights, pv[...], preferred_element_type=F32)
                summed = every[:, :HD]
                for i in range(1, kv_local):
                    summed = jnp.where(owner_o == i, every[:, i * HD:(i + 1) * HD], summed)
            outputs.append(summed * (1.0 / row_total))
            top = jnp.where(lane == g, row_max, top)
            total = jnp.where(lane == g, row_total, total)
        lse = top + jnp.log(total)
        high = lse.astype(BF16).astype(F32)
        middle = (lse - high).astype(BF16).astype(F32)
        low = lse - high - middle
        at = lax.broadcasted_iota(jnp.int32, (count, HD), 1) // 16
        outputs.append(jnp.where(at == 0, high, jnp.where(at == 1, middle, low)))
        res_out[pl.ds(first, chunk)] = jnp.concatenate(
            [o.reshape(chunk, TILE, HD) for o in outputs], axis=1).astype(BF16)

    each(1, chunk, lambda k: q_copy(k).wait_recv())
    block(0)
    each(1, chunk, lambda k: r_copy(k).start())

    def far_block(index):
        first = index * chunk
        each(0, chunk, lambda i: q_copy(first + i).wait_recv())
        block(first)
        each(0, chunk, lambda i: r_copy(first + i).start())

    each(1, n // chunk, far_block)

    def pass_on(i):
        p_copy(2 * i).wait_recv()
        p_pass(2 * i).start()

    each(1, n // 2, pass_on)

    loads[5].wait()
    loads[6].wait()
    blocks = sk.shape[2] // HD

    def wide(row):
        return jnp.concatenate([jnp.broadcast_to(row, (2 * slots, HD))] * blocks, axis=1)

    def land(k, carry):
        notes = q_tiles[k].astype(F32)[notes_at:]
        child, child_length = wide(notes[:1]), wide(notes[1:2])
        arrived = pieces[k].astype(F32)
        out = []
        for j in range(BRANCHES):
            cache, length = carry[j]
            mine = child == (base + j).astype(F32)
            out.append((jnp.where(mine, arrived, cache), jnp.where(mine, child_length, length)))
        return tuple(out)

    shape = (2 * slots, sk.shape[2])
    landed = tuple(
        (own_suffix(j), jnp.full(shape, len_ref[j].astype(F32))) for j in range(BRANCHES))
    landed = fold(0, n // 2, lambda i, c: land(2 * i, c), landed)
    p_copy(1).wait_recv()
    each(1, n // 2, lambda i: p_pass(2 * i).wait_recv())
    landed = fold(0, n // 2, lambda i, c: land(2 * i + 1, c), landed)

    slot = lax.rem(lax.broadcasted_iota(jnp.int32, shape, 0), slots).astype(F32)
    nk_all, nv_all = nk[...].astype(F32), nv[...].astype(F32)
    caches = []
    for j in range(BRANCHES):
        cache, length = landed[j]
        fresh = jnp.concatenate([
            jnp.broadcast_to(nk_all[j:j + 1], (slots, shape[1])),
            jnp.broadcast_to(nv_all[j:j + 1], (slots, shape[1]))], axis=0)
        cache = jnp.where(slot == length, fresh, cache)
        ck[j] = cache[:slots].astype(BF16)
        cv[j] = cache[slots:].astype(BF16)
        caches.append(cache)

    parts = kv_local + 1
    keys_count = BRANCHES * slots
    row_id = lax.broadcasted_iota(jnp.int32, (parts * TILE, keys_count), 0)
    key_id = lax.broadcasted_iota(jnp.int32, (parts * TILE, keys_count), 1)
    key_length = jnp.where(
        key_id[:1] >= slots, landed[1][1][:1, :keys_count], landed[0][1][:1, :keys_count])
    live = jnp.logical_and(
        lax.rem(row_id, BRANCHES) == key_id // slots,
        lax.rem(key_id, slots).astype(F32) <= jnp.broadcast_to(key_length, row_id.shape))
    own_q = q_f32[...]
    own_scores, rest_scores = [], None
    owner = lax.broadcasted_iota(jnp.int32, (TILE, HD), 0) // BRANCHES
    for g in range(kv_local):
        keys = jnp.concatenate(
            [c[:slots, g * HD:(g + 1) * HD] for c in caches], axis=0).astype(BF16)
        q = jnp.concatenate(
            [own_q[g * TILE:(g + 1) * TILE], own_q[rest:notes_at]], axis=0).astype(BF16)
        s = lax.dot_general(q, keys, NT, preferred_element_type=F32) * scale
        own_scores.append(s[:TILE])
        rest_scores = s[TILE:] if g == 0 else jnp.where(
            owner[:, :keys_count] == g, s[TILE:], rest_scores)
    scores = jnp.concatenate(own_scores + [rest_scores], axis=0)
    row_max = jnp.max(jnp.where(live, scores, -jnp.inf), axis=1, keepdims=True)
    weights = jnp.where(live, jnp.exp(scores - row_max), 0.0)
    row_total = jnp.sum(weights, axis=1, keepdims=True)
    own_sums, rest_sum = [], None
    for g in range(kv_local):
        values = jnp.concatenate(
            [c[slots:, g * HD:(g + 1) * HD] for c in caches], axis=0).astype(BF16)
        w = jnp.concatenate(
            [weights[g * TILE:(g + 1) * TILE], weights[rest:notes_at]], axis=0).astype(BF16)
        o = jnp.dot(w, values, preferred_element_type=F32)
        own_sums.append(o[:TILE])
        rest_sum = o[TILE:] if g == 0 else jnp.where(owner == g, o[TILE:], rest_sum)
    own_sums.append(rest_sum)
    lane = lax.broadcasted_iota(jnp.int32, (TILE, HD), 1)
    own_top = jnp.zeros((TILE, HD), F32)
    own_total = jnp.ones((TILE, HD), F32)
    for g in range(parts):
        at = slice(g * TILE, (g + 1) * TILE)
        own_top = jnp.where(lane == g, row_max[at], own_top)
        own_total = jnp.where(lane == g, row_total[at], own_total)

    def lse_of(tile):
        terms = tile.astype(F32)[notes_at:]
        return terms + pltpu.roll(terms, HD - 16, 1) + pltpu.roll(terms, HD - 32, 1)

    def highest(k, m):
        return jnp.maximum(m, lse_of(res_in[k]))

    def add(tile, best, carry):
        sums, total = carry
        factor = jnp.exp(lse_of(tile) - best)
        tile = tile.astype(F32)
        sums = tuple(
            s + tile[g * TILE:(g + 1) * TILE] * factor[:, g:g + 1] for g, s in enumerate(sums))
        return sums, total + factor

    def scaled(factor, sums, total):
        return tuple(s * factor[:, g:g + 1] for g, s in enumerate(sums)), total * factor

    each(1, chunk, lambda k: r_copy(k).wait_recv())
    near = fold(1, chunk, highest, jnp.maximum(own_top, lse_of(res_out[0])))
    carry = scaled(jnp.exp(own_top - near), own_sums, own_total)
    carry = add(res_out[0], near, carry)
    carry = fold(1, chunk, lambda k, c: add(res_in[k], near, c), carry)
    each(chunk, n, lambda k: r_copy(k).wait_recv())
    best = fold(chunk, n, highest, near)
    carry = scaled(jnp.exp(near - best), *carry)
    sums, total = fold(chunk, n, lambda k, c: add(res_in[k], best, c), carry)
    for g in range(parts):
        att_rows[g * TILE:(g + 1) * TILE, :] = sums[g] / total[:, g:g + 1]
    att[...] = jnp.concatenate(
        [att_rows[row_of(g, h):row_of(g, h) + BRANCHES, :]
         for g in range(kv_local) for h in range(GROUP)], axis=1).astype(BF16)

    def drain(k):
        q_copy(k).wait_send()
        r_copy(k).wait_send()

    def drain_pieces(i):
        p_copy(2 * i).wait_send()
        p_pass(2 * i).wait_send()

    each(1, n, drain)
    p_copy(1).wait_send()
    each(1, n // 2, drain_pieces)


def place(*refs):
    count = len(refs) // 2
    sems = refs[-1]
    copies = [
        pltpu.make_async_copy(refs[i], refs[count + i], sems.at[i]) for i in range(count)]
    for item in copies:
        item.start()
    for item in copies:
        item.wait()


def shards(n, *args):
    queries, prefix_keys, prefix_values, suffix_keys, suffix_values = args[:5]
    new_keys, new_values, suffix_lengths, fork_list = args[5:]
    slots, width = suffix_keys.shape[1:]
    kv_local = width // HD
    rows = (kv_local + 2) * TILE
    assert queries.shape[0] == BRANCHES and fork_list.shape[0] == 1
    assert n * BRANCHES <= 256 and rows % 16 == 0 and n & (n - 1) == 0
    dma = pltpu.SemaphoreType.DMA
    hbm_spec = pl.BlockSpec(memory_space=pltpu.HBM)
    vmem_spec = pl.BlockSpec(memory_space=pltpu.VMEM)
    like = lambda x: pltpu.VMEM(x.shape, x.dtype)
    out_shape = (
        jax.ShapeDtypeStruct(queries.shape, BF16),
        jax.ShapeDtypeStruct(suffix_keys.shape, BF16),
        jax.ShapeDtypeStruct(suffix_values.shape, BF16),
    )
    results = pl.pallas_call(
        functools.partial(kernel, n),
        out_shape=out_shape,
        in_specs=[hbm_spec] * 9,
        out_specs=(vmem_spec,) * 3,
        scratch_shapes=[
            like(queries), like(prefix_keys), like(prefix_values), like(suffix_keys),
            like(suffix_values), like(new_keys), like(new_values),
            pltpu.SMEM(suffix_lengths.shape, jnp.int32), pltpu.SMEM(fork_list.shape, jnp.int32),
            pltpu.VMEM((rows, HD), F32),
            pltpu.VMEM((n, rows, HD), BF16),
            pltpu.VMEM((n, 2 * slots, width), BF16),
            pltpu.VMEM((n, rows, HD), BF16),
            pltpu.VMEM((n, rows, HD), BF16),
            pltpu.VMEM((rows, HD), F32),
            dma((9,)),
        ] + [dma((n,))] * 6,
        compiler_params=pltpu.CompilerParams(
            collective_id=0, has_side_effects=True, vmem_limit_bytes=32 * 2**20),
    )(*[pltpu.with_memory_space_constraint(x, pltpu.HBM) for x in args])
    return pl.pallas_call(
        place,
        out_shape=out_shape,
        in_specs=[vmem_spec] * 3,
        out_specs=(hbm_spec,) * 3,
        scratch_shapes=[dma((3,))],
        compiler_params=pltpu.CompilerParams(vmem_limit_bytes=2**20),
    )(*results)


def solution(mesh):
    return jax.shard_map(
        functools.partial(shards, mesh.shape["seq"]),
        mesh=mesh,
        in_specs=(
            P(("groups", "seq"), "mp"),
            P(("groups", "seq"), "mp"),
            P(("groups", "seq"), "mp"),
            P(("groups", "seq"), None, "mp"),
            P(("groups", "seq"), None, "mp"),
            P(("groups", "seq"), "mp"),
            P(("groups", "seq"), "mp"),
            P(("groups", "seq")),
            P(("groups", "seq"), None),
        ),
        out_specs=(
            P(("groups", "seq"), "mp"),
            P(("groups", "seq"), None, "mp"),
            P(("groups", "seq"), None, "mp"),
        ),
        check_vma=False,
    )
```

```python
import functools
import math

import jax
import jax.numpy as jnp
from jax import lax
from jax.experimental import pallas as pl
from jax.experimental.pallas import tpu as pltpu
from jax.sharding import PartitionSpec as P

HQ = 40
KVH = 8
HD = 128
GROUP = HQ // KVH
BRANCHES = 2
TILE = 8
MESH = pl.DeviceIdType.MESH
NT = (((1,), (1,)), ((), ()))
UNROLL_UP_TO = 16
F32 = jnp.float32
BF16 = jnp.bfloat16


def each(start, stop, body):
    if stop - start <= UNROLL_UP_TO:
        for index in range(start, stop):
            body(index)
    else:
        def step(index, carry):
            body(index)
            return carry

        lax.fori_loop(start, stop, step, 0)


def fold(start, stop, body, carry):
    if stop - start <= UNROLL_UP_TO:
        for index in range(start, stop):
            carry = body(index, carry)
        return carry
    return lax.fori_loop(start, stop, body, carry)


def kernel(
    n,
    q_hbm, pk_hbm, pv_hbm, sk_hbm, sv_hbm, nk_hbm, nv_hbm, len_hbm, fork_hbm,
    att, ck, cv,
    q_in, pk, pv, sk, sv, nk, nv, len_ref, fork_ref,
    q_f32, q_tiles, pieces, res_out, res_in, att_rows,
    in_sem, q_send, q_recv, p_send, p_recv, r_send, r_recv,
):
    me = lax.axis_index("seq")
    slots = sk.shape[1]
    kv_local = pk.shape[1] // HD
    scale = 1.0 / math.sqrt(HD)
    base = me * BRANCHES
    rest = kv_local * TILE
    notes_at = rest + TILE
    chunk = math.gcd(n, 4)

    def partner(k):
        other, bit = me, 1
        while bit < n:
            other = other + (k // bit) % 2 * bit * (1 - 2 * ((me // bit) % 2))
            bit *= 2
        return {"seq": other}

    barrier = pltpu.get_barrier_semaphore()
    each(1, n, lambda k: pl.semaphore_signal(
        barrier, inc=1, device_id=partner(k), device_id_type=MESH))

    loads = [
        pltpu.make_async_copy(src, dst, in_sem.at[i])
        for i, (src, dst) in enumerate([
            (q_hbm, q_in), (sk_hbm, sk), (sv_hbm, sv), (pk_hbm, pk),
            (pv_hbm, pv), (nk_hbm, nk), (nv_hbm, nv), (len_hbm, len_ref), (fork_hbm, fork_ref)])
    ]
    for i in (0, 7, 8, 1, 2, 3, 4, 5, 6):
        loads[i].start()

    def row_of(g, h):
        return g * TILE + h * BRANCHES if h < GROUP - 1 else rest + g * BRANCHES

    loads[7].wait()
    loads[8].wait()
    parent = fork_ref[0, 0] - base
    parent_length = jnp.where(parent == 0, len_ref[0], len_ref[1])
    q_f32[notes_at:] = jnp.zeros((TILE, HD), F32)
    q_f32[notes_at:notes_at + 1] = jnp.full((1, HD), fork_ref[0, 1].astype(F32))
    q_f32[notes_at + 1:notes_at + 2] = jnp.full((1, HD), parent_length.astype(F32))
    loads[0].wait()
    q_all = q_in[...].astype(F32)
    for g in range(kv_local):
        for h in range(GROUP):
            at = (g * GROUP + h) * HD
            q_f32[row_of(g, h):row_of(g, h) + BRANCHES, :] = q_all[:, at:at + HD]
    q_tiles[0] = q_f32[...].astype(BF16)

    loads[1].wait()
    loads[2].wait()

    def own_suffix(j):
        return jnp.concatenate([sk[j].astype(F32), sv[j].astype(F32)], axis=0)

    parent_b = jnp.full((2 * slots, sk.shape[2]), parent.astype(F32))
    pieces[0] = jnp.where(parent_b == 0.0, own_suffix(0), own_suffix(1)).astype(BF16)

    pl.semaphore_wait(barrier, n - 1)

    def copy(src, dst, send, recv, k):
        return pltpu.make_async_remote_copy(
            src_ref=src, dst_ref=dst, send_sem=send.at[k], recv_sem=recv.at[k],
            device_id=partner(k), device_id_type=MESH)

    def q_copy(k):
        return copy(q_tiles.at[0], q_tiles.at[k], q_send, q_recv, k)

    def p_copy(k):
        return copy(pieces.at[0], pieces.at[k], p_send, p_recv, k)

    def p_pass(k):
        return pltpu.make_async_remote_copy(
            src_ref=pieces.at[k], dst_ref=pieces.at[k + 1],
            send_sem=p_send.at[k + 1], recv_sem=p_recv.at[k + 1],
            device_id=partner(1), device_id_type=MESH)

    def r_copy(k):
        return copy(res_out.at[k], res_in.at[k], r_send, r_recv, k)

    def far_first(body):
        each(chunk, n, body)
        each(1, chunk, body)

    far_first(lambda k: q_copy(k).start())

    loads[3].wait()
    loads[4].wait()

    count = chunk * TILE
    lane = lax.rem(lax.broadcasted_iota(jnp.int32, (count, HD), 1), 16)
    owner_s = lax.rem(lax.broadcasted_iota(jnp.int32, (count, pk.shape[0]), 0), TILE) // BRANCHES
    owner_o = lax.rem(lax.broadcasted_iota(jnp.int32, (count, HD), 0), TILE) // BRANCHES

    def softmax(scores):
        row_max = jnp.max(scores, axis=1, keepdims=True)
        weights = jnp.exp(scores - row_max)
        return row_max, jnp.sum(weights, axis=1, keepdims=True), weights.astype(BF16)

    def block(first):
        tiles = q_tiles[pl.ds(first, chunk)].astype(F32)

        def rows(at):
            return tiles[:, at:at + TILE].reshape(count, HD)

        last = rows(rest)
        scores, rest_scores = [], None
        for g in range(kv_local):
            q = jnp.concatenate([rows(g * TILE), last], axis=0).astype(BF16)
            s = lax.dot_general(
                q, pk[:, g * HD:(g + 1) * HD], NT, preferred_element_type=F32) * scale
            scores.append(s[:count])
            rest_scores = s[count:] if g == 0 else jnp.where(owner_s == g, s[count:], rest_scores)
        outputs = []
        top = jnp.zeros((count, HD), F32)
        total = jnp.ones((count, HD), F32)
        for g, s in enumerate(scores + [rest_scores]):
            row_max, row_total, weights = softmax(s)
            if g < kv_local:
                summed = jnp.dot(
                    weights, pv[:, g * HD:(g + 1) * HD], preferred_element_type=F32)
            else:
                every = jnp.dot(weights, pv[...], preferred_element_type=F32)
                summed = every[:, :HD]
                for i in range(1, kv_local):
                    summed = jnp.where(owner_o == i, every[:, i * HD:(i + 1) * HD], summed)
            outputs.append(summed * (1.0 / row_total))
            top = jnp.where(lane == g, row_max, top)
            total = jnp.where(lane == g, row_total, total)
        lse = top + jnp.log(total)
        high = lse.astype(BF16).astype(F32)
        middle = (lse - high).astype(BF16).astype(F32)
        low = lse - high - middle
        at = lax.broadcasted_iota(jnp.int32, (count, HD), 1) // 16
        outputs.append(jnp.where(at == 0, high, jnp.where(at == 1, middle, low)))
        res_out[pl.ds(first, chunk)] = jnp.concatenate(
            [o.reshape(chunk, TILE, HD) for o in outputs], axis=1).astype(BF16)

    each(1, chunk, lambda k: q_copy(k).wait_recv())
    block(0)
    each(1, chunk, lambda k: r_copy(k).start())
    each(1, n // 2, lambda i: p_copy(n - 2 * i).start())
    p_copy(1).start()

    def far_block(index):
        first = index * chunk
        each(0, chunk, lambda i: q_copy(first + i).wait_recv())
        block(first)
        each(0, chunk, lambda i: r_copy(first + i).start())

    each(1, n // chunk, far_block)

    def pass_on(i):
        p_copy(2 * i).wait_recv()
        p_pass(2 * i).start()

    each(1, n // 2, pass_on)

    loads[5].wait()
    loads[6].wait()
    blocks = sk.shape[2] // HD

    def wide(row):
        return jnp.concatenate([jnp.broadcast_to(row, (2 * slots, HD))] * blocks, axis=1)

    def land(k, carry):
        notes = q_tiles[k].astype(F32)[notes_at:]
        child, child_length = wide(notes[:1]), wide(notes[1:2])
        arrived = pieces[k].astype(F32)
        out = []
        for j in range(BRANCHES):
            cache, length = carry[j]
            mine = child == (base + j).astype(F32)
            out.append((jnp.where(mine, arrived, cache), jnp.where(mine, child_length, length)))
        return tuple(out)

    shape = (2 * slots, sk.shape[2])
    landed = tuple(
        (own_suffix(j), jnp.full(shape, len_ref[j].astype(F32))) for j in range(BRANCHES))
    landed = fold(0, n // 2, lambda i, c: land(2 * i, c), landed)
    p_copy(1).wait_recv()
    each(1, n // 2, lambda i: p_pass(2 * i).wait_recv())
    landed = fold(0, n // 2, lambda i, c: land(2 * i + 1, c), landed)

    slot = lax.rem(lax.broadcasted_iota(jnp.int32, shape, 0), slots).astype(F32)
    nk_all, nv_all = nk[...].astype(F32), nv[...].astype(F32)
    caches = []
    for j in range(BRANCHES):
        cache, length = landed[j]
        fresh = jnp.concatenate([
            jnp.broadcast_to(nk_all[j:j + 1], (slots, shape[1])),
            jnp.broadcast_to(nv_all[j:j + 1], (slots, shape[1]))], axis=0)
        cache = jnp.where(slot == length, fresh, cache)
        ck[j] = cache[:slots].astype(BF16)
        cv[j] = cache[slots:].astype(BF16)
        caches.append(cache)

    parts = kv_local + 1
    keys_count = BRANCHES * slots
    row_id = lax.broadcasted_iota(jnp.int32, (parts * TILE, keys_count), 0)
    key_id = lax.broadcasted_iota(jnp.int32, (parts * TILE, keys_count), 1)
    key_length = jnp.where(
        key_id[:1] >= slots, landed[1][1][:1, :keys_count], landed[0][1][:1, :keys_count])
    live = jnp.logical_and(
        lax.rem(row_id, BRANCHES) == key_id // slots,
        lax.rem(key_id, slots).astype(F32) <= jnp.broadcast_to(key_length, row_id.shape))
    own_q = q_f32[...]
    own_scores, rest_scores = [], None
    owner = lax.broadcasted_iota(jnp.int32, (TILE, HD), 0) // BRANCHES
    for g in range(kv_local):
        keys = jnp.concatenate(
            [c[:slots, g * HD:(g + 1) * HD] for c in caches], axis=0).astype(BF16)
        q = jnp.concatenate(
            [own_q[g * TILE:(g + 1) * TILE], own_q[rest:notes_at]], axis=0).astype(BF16)
        s = lax.dot_general(q, keys, NT, preferred_element_type=F32) * scale
        own_scores.append(s[:TILE])
        rest_scores = s[TILE:] if g == 0 else jnp.where(
            owner[:, :keys_count] == g, s[TILE:], rest_scores)
    scores = jnp.concatenate(own_scores + [rest_scores], axis=0)
    row_max = jnp.max(jnp.where(live, scores, -jnp.inf), axis=1, keepdims=True)
    weights = jnp.where(live, jnp.exp(scores - row_max), 0.0)
    row_total = jnp.sum(weights, axis=1, keepdims=True)
    own_sums, rest_sum = [], None
    for g in range(kv_local):
        values = jnp.concatenate(
            [c[slots:, g * HD:(g + 1) * HD] for c in caches], axis=0).astype(BF16)
        w = jnp.concatenate(
            [weights[g * TILE:(g + 1) * TILE], weights[rest:notes_at]], axis=0).astype(BF16)
        o = jnp.dot(w, values, preferred_element_type=F32)
        own_sums.append(o[:TILE])
        rest_sum = o[TILE:] if g == 0 else jnp.where(owner == g, o[TILE:], rest_sum)
    own_sums.append(rest_sum)
    lane = lax.broadcasted_iota(jnp.int32, (TILE, HD), 1)
    own_top = jnp.zeros((TILE, HD), F32)
    own_total = jnp.ones((TILE, HD), F32)
    for g in range(parts):
        at = slice(g * TILE, (g + 1) * TILE)
        own_top = jnp.where(lane == g, row_max[at], own_top)
        own_total = jnp.where(lane == g, row_total[at], own_total)

    def lse_of(tile):
        terms = tile.astype(F32)[notes_at:]
        return terms + pltpu.roll(terms, HD - 16, 1) + pltpu.roll(terms, HD - 32, 1)

    def highest(k, m):
        return jnp.maximum(m, lse_of(res_in[k]))

    def add(tile, best, carry):
        sums, total = carry
        factor = jnp.exp(lse_of(tile) - best)
        tile = tile.astype(F32)
        sums = tuple(
            s + tile[g * TILE:(g + 1) * TILE] * factor[:, g:g + 1] for g, s in enumerate(sums))
        return sums, total + factor

    def scaled(factor, sums, total):
        return tuple(s * factor[:, g:g + 1] for g, s in enumerate(sums)), total * factor

    each(1, chunk, lambda k: r_copy(k).wait_recv())
    near = fold(1, chunk, highest, jnp.maximum(own_top, lse_of(res_out[0])))
    carry = scaled(jnp.exp(own_top - near), own_sums, own_total)
    carry = add(res_out[0], near, carry)
    carry = fold(1, chunk, lambda k, c: add(res_in[k], near, c), carry)
    each(chunk, n, lambda k: r_copy(k).wait_recv())
    best = fold(chunk, n, highest, near)
    carry = scaled(jnp.exp(near - best), *carry)
    sums, total = fold(chunk, n, lambda k, c: add(res_in[k], best, c), carry)
    for g in range(parts):
        att_rows[g * TILE:(g + 1) * TILE, :] = sums[g] / total[:, g:g + 1]
    att[...] = jnp.concatenate(
        [att_rows[row_of(g, h):row_of(g, h) + BRANCHES, :]
         for g in range(kv_local) for h in range(GROUP)], axis=1).astype(BF16)

    def drain(k):
        q_copy(k).wait_send()
        r_copy(k).wait_send()

    def drain_pieces(i):
        p_copy(2 * i).wait_send()
        p_pass(2 * i).wait_send()

    each(1, n, drain)
    p_copy(1).wait_send()
    each(1, n // 2, drain_pieces)


def place(*refs):
    count = len(refs) // 2
    sems = refs[-1]
    copies = [
        pltpu.make_async_copy(refs[i], refs[count + i], sems.at[i]) for i in range(count)]
    for item in copies:
        item.start()
    for item in copies:
        item.wait()


def shards(n, *args):
    queries, prefix_keys, prefix_values, suffix_keys, suffix_values = args[:5]
    new_keys, new_values, suffix_lengths, fork_list = args[5:]
    slots, width = suffix_keys.shape[1:]
    kv_local = width // HD
    rows = (kv_local + 2) * TILE
    assert queries.shape[0] == BRANCHES and fork_list.shape[0] == 1
    assert n * BRANCHES <= 256 and rows % 16 == 0 and n & (n - 1) == 0
    dma = pltpu.SemaphoreType.DMA
    hbm_spec = pl.BlockSpec(memory_space=pltpu.HBM)
    vmem_spec = pl.BlockSpec(memory_space=pltpu.VMEM)
    like = lambda x: pltpu.VMEM(x.shape, x.dtype)
    out_shape = (
        jax.ShapeDtypeStruct(queries.shape, BF16),
        jax.ShapeDtypeStruct(suffix_keys.shape, BF16),
        jax.ShapeDtypeStruct(suffix_values.shape, BF16),
    )
    results = pl.pallas_call(
        functools.partial(kernel, n),
        out_shape=out_shape,
        in_specs=[hbm_spec] * 9,
        out_specs=(vmem_spec,) * 3,
        scratch_shapes=[
            like(queries), like(prefix_keys), like(prefix_values), like(suffix_keys),
            like(suffix_values), like(new_keys), like(new_values),
            pltpu.SMEM(suffix_lengths.shape, jnp.int32), pltpu.SMEM(fork_list.shape, jnp.int32),
            pltpu.VMEM((rows, HD), F32),
            pltpu.VMEM((n, rows, HD), BF16),
            pltpu.VMEM((n, 2 * slots, width), BF16),
            pltpu.VMEM((n, rows, HD), BF16),
            pltpu.VMEM((n, rows, HD), BF16),
            pltpu.VMEM((rows, HD), F32),
            dma((9,)),
        ] + [dma((n,))] * 6,
        compiler_params=pltpu.CompilerParams(
            collective_id=0, has_side_effects=True, vmem_limit_bytes=32 * 2**20),
    )(*[pltpu.with_memory_space_constraint(x, pltpu.HBM) for x in args])
    return pl.pallas_call(
        place,
        out_shape=out_shape,
        in_specs=[vmem_spec] * 3,
        out_specs=(hbm_spec,) * 3,
        scratch_shapes=[dma((3,))],
        compiler_params=pltpu.CompilerParams(vmem_limit_bytes=2**20),
    )(*results)


def solution(mesh):
    return jax.shard_map(
        functools.partial(shards, mesh.shape["seq"]),
        mesh=mesh,
        in_specs=(
            P(("groups", "seq"), "mp"),
            P(("groups", "seq"), "mp"),
            P(("groups", "seq"), "mp"),
            P(("groups", "seq"), None, "mp"),
            P(("groups", "seq"), None, "mp"),
            P(("groups", "seq"), "mp"),
            P(("groups", "seq"), "mp"),
            P(("groups", "seq")),
            P(("groups", "seq"), None),
        ),
        out_specs=(
            P(("groups", "seq"), "mp"),
            P(("groups", "seq"), None, "mp"),
            P(("groups", "seq"), None, "mp"),
        ),
        check_vma=False,
    )
```

```python
import functools
import math

import jax
import jax.numpy as jnp
from jax import lax
from jax.experimental import pallas as pl
from jax.experimental.pallas import tpu as pltpu
from jax.sharding import PartitionSpec as P

HQ = 40
KVH = 8
HD = 128
GROUP = HQ // KVH
BRANCHES = 2
TILE = 8
MESH = pl.DeviceIdType.MESH
NT = (((1,), (1,)), ((), ()))
UNROLL_UP_TO = 16
F32 = jnp.float32
BF16 = jnp.bfloat16


def each(start, stop, body):
    if stop - start <= UNROLL_UP_TO:
        for index in range(start, stop):
            body(index)
    else:
        def step(index, carry):
            body(index)
            return carry

        lax.fori_loop(start, stop, step, 0)


def fold(start, stop, body, carry):
    if stop - start <= UNROLL_UP_TO:
        for index in range(start, stop):
            carry = body(index, carry)
        return carry
    return lax.fori_loop(start, stop, body, carry)


def kernel(
    n,
    q_hbm, pk_hbm, pv_hbm, sk_hbm, sv_hbm, nk_hbm, nv_hbm, len_hbm, fork_hbm,
    att, ck, cv,
    q_in, pk, pv, sk, sv, nk, nv, len_ref, fork_ref,
    q_f32, q_tiles, pieces, res_out, res_in, att_rows,
    in_sem, q_send, q_recv, p_send, p_recv, r_send, r_recv,
):
    me = lax.axis_index("seq")
    slots = sk.shape[1]
    kv_local = pk.shape[1] // HD
    scale = 1.0 / math.sqrt(HD)
    base = me * BRANCHES
    rest = kv_local * TILE
    notes_at = rest + TILE
    chunk = math.gcd(n, 4)

    def partner(k):
        other, bit = me, 1
        while bit < n:
            other = other + (k // bit) % 2 * bit * (1 - 2 * ((me // bit) % 2))
            bit *= 2
        return {"seq": other}

    barrier = pltpu.get_barrier_semaphore()
    each(1, n, lambda k: pl.semaphore_signal(
        barrier, inc=1, device_id=partner(k), device_id_type=MESH))

    loads = [
        pltpu.make_async_copy(src, dst, in_sem.at[i])
        for i, (src, dst) in enumerate([
            (q_hbm, q_in), (sk_hbm, sk), (sv_hbm, sv), (pk_hbm, pk),
            (pv_hbm, pv), (nk_hbm, nk), (nv_hbm, nv), (len_hbm, len_ref), (fork_hbm, fork_ref)])
    ]
    for i in (0, 7, 8, 1, 2, 3, 4, 5, 6):
        loads[i].start()

    def row_of(g, h):
        return g * TILE + h * BRANCHES if h < GROUP - 1 else rest + g * BRANCHES

    loads[7].wait()
    loads[8].wait()
    parent = fork_ref[0, 0] - base
    parent_length = jnp.where(parent == 0, len_ref[0], len_ref[1])
    q_f32[notes_at:] = jnp.zeros((TILE, HD), F32)
    q_f32[notes_at:notes_at + 1] = jnp.full((1, HD), fork_ref[0, 1].astype(F32))
    q_f32[notes_at + 1:notes_at + 2] = jnp.full((1, HD), parent_length.astype(F32))
    loads[0].wait()
    q_all = q_in[...].astype(F32)
    for g in range(kv_local):
        for h in range(GROUP):
            at = (g * GROUP + h) * HD
            q_f32[row_of(g, h):row_of(g, h) + BRANCHES, :] = q_all[:, at:at + HD]
    q_tiles[0] = q_f32[...].astype(BF16)

    loads[1].wait()
    loads[2].wait()

    def own_suffix(j):
        return jnp.concatenate([sk[j].astype(F32), sv[j].astype(F32)], axis=0)

    parent_b = jnp.full((2 * slots, sk.shape[2]), parent.astype(F32))
    pieces[0] = jnp.where(parent_b == 0.0, own_suffix(0), own_suffix(1)).astype(BF16)

    pl.semaphore_wait(barrier, n - 1)

    def copy(src, dst, send, recv, k):
        return pltpu.make_async_remote_copy(
            src_ref=src, dst_ref=dst, send_sem=send.at[k], recv_sem=recv.at[k],
            device_id=partner(k), device_id_type=MESH)

    def q_copy(k):
        return copy(q_tiles.at[0], q_tiles.at[k], q_send, q_recv, k)

    def p_copy(k):
        return copy(pieces.at[0], pieces.at[k], p_send, p_recv, k)

    def p_pass(k):
        return pltpu.make_async_remote_copy(
            src_ref=pieces.at[k], dst_ref=pieces.at[k + 1],
            send_sem=p_send.at[k + 1], recv_sem=p_recv.at[k + 1],
            device_id=partner(1), device_id_type=MESH)

    def r_copy(k):
        return copy(res_out.at[k], res_in.at[k], r_send, r_recv, k)

    def far_first(body):
        each(chunk, n, body)
        each(1, chunk, body)

    far_first(lambda k: q_copy(k).start())
    each(1, n // 2, lambda i: p_copy(n - 2 * i).start())
    p_copy(1).start()

    loads[3].wait()
    loads[4].wait()

    count = chunk * TILE
    lane = lax.rem(lax.broadcasted_iota(jnp.int32, (count, HD), 1), 16)
    owner_s = lax.rem(lax.broadcasted_iota(jnp.int32, (count, pk.shape[0]), 0), TILE) // BRANCHES
    owner_o = lax.rem(lax.broadcasted_iota(jnp.int32, (count, HD), 0), TILE) // BRANCHES

    def softmax(scores):
        row_max = jnp.max(scores, axis=1, keepdims=True)
        weights = jnp.exp(scores - row_max)
        return row_max, jnp.sum(weights, axis=1, keepdims=True), weights.astype(BF16)

    def block(first):
        tiles = q_tiles[pl.ds(first, chunk)].astype(F32)

        def rows(at):
            return tiles[:, at:at + TILE].reshape(count, HD)

        last = rows(rest)
        scores, rest_scores = [], None
        for g in range(kv_local):
            q = jnp.concatenate([rows(g * TILE), last], axis=0).astype(BF16)
            s = lax.dot_general(
                q, pk[:, g * HD:(g + 1) * HD], NT, preferred_element_type=F32) * scale
            scores.append(s[:count])
            rest_scores = s[count:] if g == 0 else jnp.where(owner_s == g, s[count:], rest_scores)
        outputs = []
        top = jnp.zeros((count, HD), F32)
        total = jnp.ones((count, HD), F32)
        for g, s in enumerate(scores + [rest_scores]):
            row_max, row_total, weights = softmax(s)
            if g < kv_local:
                summed = jnp.dot(
                    weights, pv[:, g * HD:(g + 1) * HD], preferred_element_type=F32)
            else:
                every = jnp.dot(weights, pv[...], preferred_element_type=F32)
                summed = every[:, :HD]
                for i in range(1, kv_local):
                    summed = jnp.where(owner_o == i, every[:, i * HD:(i + 1) * HD], summed)
            outputs.append(summed * (1.0 / row_total))
            top = jnp.where(lane == g, row_max, top)
            total = jnp.where(lane == g, row_total, total)
        lse = top + jnp.log(total)
        high = lse.astype(BF16).astype(F32)
        middle = (lse - high).astype(BF16).astype(F32)
        low = lse - high - middle
        at = lax.broadcasted_iota(jnp.int32, (count, HD), 1) // 16
        outputs.append(jnp.where(at == 0, high, jnp.where(at == 1, middle, low)))
        res_out[pl.ds(first, chunk)] = jnp.concatenate(
            [o.reshape(chunk, TILE, HD) for o in outputs], axis=1).astype(BF16)

    each(1, chunk, lambda k: q_copy(k).wait_recv())
    block(0)
    each(1, chunk, lambda k: r_copy(k).start())

    def pass_on(i):
        p_copy(2 * i).wait_recv()
        p_pass(2 * i).start()

    each(1, n // 2, pass_on)

    def far_block(index):
        first = index * chunk
        each(0, chunk, lambda i: q_copy(first + i).wait_recv())
        block(first)
        each(0, chunk, lambda i: r_copy(first + i).start())

    each(1, n // chunk, far_block)

    loads[5].wait()
    loads[6].wait()
    blocks = sk.shape[2] // HD

    def wide(row):
        return jnp.concatenate([jnp.broadcast_to(row, (2 * slots, HD))] * blocks, axis=1)

    def land(k, carry):
        notes = q_tiles[k].astype(F32)[notes_at:]
        child, child_length = wide(notes[:1]), wide(notes[1:2])
        arrived = pieces[k].astype(F32)
        out = []
        for j in range(BRANCHES):
            cache, length = carry[j]
            mine = child == (base + j).astype(F32)
            out.append((jnp.where(mine, arrived, cache), jnp.where(mine, child_length, length)))
        return tuple(out)

    shape = (2 * slots, sk.shape[2])
    landed = tuple(
        (own_suffix(j), jnp.full(shape, len_ref[j].astype(F32))) for j in range(BRANCHES))
    landed = fold(0, n // 2, lambda i, c: land(2 * i, c), landed)
    p_copy(1).wait_recv()
    each(1, n // 2, lambda i: p_pass(2 * i).wait_recv())
    landed = fold(0, n // 2, lambda i, c: land(2 * i + 1, c), landed)

    slot = lax.rem(lax.broadcasted_iota(jnp.int32, shape, 0), slots).astype(F32)
    nk_all, nv_all = nk[...].astype(F32), nv[...].astype(F32)
    caches = []
    for j in range(BRANCHES):
        cache, length = landed[j]
        fresh = jnp.concatenate([
            jnp.broadcast_to(nk_all[j:j + 1], (slots, shape[1])),
            jnp.broadcast_to(nv_all[j:j + 1], (slots, shape[1]))], axis=0)
        cache = jnp.where(slot == length, fresh, cache)
        ck[j] = cache[:slots].astype(BF16)
        cv[j] = cache[slots:].astype(BF16)
        caches.append(cache)

    parts = kv_local + 1
    keys_count = BRANCHES * slots
    row_id = lax.broadcasted_iota(jnp.int32, (parts * TILE, keys_count), 0)
    key_id = lax.broadcasted_iota(jnp.int32, (parts * TILE, keys_count), 1)
    key_length = jnp.where(
        key_id[:1] >= slots, landed[1][1][:1, :keys_count], landed[0][1][:1, :keys_count])
    live = jnp.logical_and(
        lax.rem(row_id, BRANCHES) == key_id // slots,
        lax.rem(key_id, slots).astype(F32) <= jnp.broadcast_to(key_length, row_id.shape))
    own_q = q_f32[...]
    own_scores, rest_scores = [], None
    owner = lax.broadcasted_iota(jnp.int32, (TILE, HD), 0) // BRANCHES
    for g in range(kv_local):
        keys = jnp.concatenate(
            [c[:slots, g * HD:(g + 1) * HD] for c in caches], axis=0).astype(BF16)
        q = jnp.concatenate(
            [own_q[g * TILE:(g + 1) * TILE], own_q[rest:notes_at]], axis=0).astype(BF16)
        s = lax.dot_general(q, keys, NT, preferred_element_type=F32) * scale
        own_scores.append(s[:TILE])
        rest_scores = s[TILE:] if g == 0 else jnp.where(
            owner[:, :keys_count] == g, s[TILE:], rest_scores)
    scores = jnp.concatenate(own_scores + [rest_scores], axis=0)
    row_max = jnp.max(jnp.where(live, scores, -jnp.inf), axis=1, keepdims=True)
    weights = jnp.where(live, jnp.exp(scores - row_max), 0.0)
    row_total = jnp.sum(weights, axis=1, keepdims=True)
    own_sums, rest_sum = [], None
    for g in range(kv_local):
        values = jnp.concatenate(
            [c[slots:, g * HD:(g + 1) * HD] for c in caches], axis=0).astype(BF16)
        w = jnp.concatenate(
            [weights[g * TILE:(g + 1) * TILE], weights[rest:notes_at]], axis=0).astype(BF16)
        o = jnp.dot(w, values, preferred_element_type=F32)
        own_sums.append(o[:TILE])
        rest_sum = o[TILE:] if g == 0 else jnp.where(owner == g, o[TILE:], rest_sum)
    own_sums.append(rest_sum)
    lane = lax.broadcasted_iota(jnp.int32, (TILE, HD), 1)
    own_top = jnp.zeros((TILE, HD), F32)
    own_total = jnp.ones((TILE, HD), F32)
    for g in range(parts):
        at = slice(g * TILE, (g + 1) * TILE)
        own_top = jnp.where(lane == g, row_max[at], own_top)
        own_total = jnp.where(lane == g, row_total[at], own_total)

    def lse_of(tile):
        terms = tile.astype(F32)[notes_at:]
        return terms + pltpu.roll(terms, HD - 16, 1) + pltpu.roll(terms, HD - 32, 1)

    def highest(k, m):
        return jnp.maximum(m, lse_of(res_in[k]))

    def add(tile, best, carry):
        sums, total = carry
        factor = jnp.exp(lse_of(tile) - best)
        tile = tile.astype(F32)
        sums = tuple(
            s + tile[g * TILE:(g + 1) * TILE] * factor[:, g:g + 1] for g, s in enumerate(sums))
        return sums, total + factor

    def scaled(factor, sums, total):
        return tuple(s * factor[:, g:g + 1] for g, s in enumerate(sums)), total * factor

    each(1, chunk, lambda k: r_copy(k).wait_recv())
    near = fold(1, chunk, highest, jnp.maximum(own_top, lse_of(res_out[0])))
    carry = scaled(jnp.exp(own_top - near), own_sums, own_total)
    carry = add(res_out[0], near, carry)
    carry = fold(1, chunk, lambda k, c: add(res_in[k], near, c), carry)
    each(chunk, n, lambda k: r_copy(k).wait_recv())
    best = fold(chunk, n, highest, near)
    carry = scaled(jnp.exp(near - best), *carry)
    sums, total = fold(chunk, n, lambda k, c: add(res_in[k], best, c), carry)
    for g in range(parts):
        att_rows[g * TILE:(g + 1) * TILE, :] = sums[g] / total[:, g:g + 1]
    att[...] = jnp.concatenate(
        [att_rows[row_of(g, h):row_of(g, h) + BRANCHES, :]
         for g in range(kv_local) for h in range(GROUP)], axis=1).astype(BF16)

    def drain(k):
        q_copy(k).wait_send()
        r_copy(k).wait_send()

    def drain_pieces(i):
        p_copy(2 * i).wait_send()
        p_pass(2 * i).wait_send()

    each(1, n, drain)
    p_copy(1).wait_send()
    each(1, n // 2, drain_pieces)


def place(*refs):
    count = len(refs) // 2
    sems = refs[-1]
    copies = [
        pltpu.make_async_copy(refs[i], refs[count + i], sems.at[i]) for i in range(count)]
    for item in copies:
        item.start()
    for item in copies:
        item.wait()


def shards(n, *args):
    queries, prefix_keys, prefix_values, suffix_keys, suffix_values = args[:5]
    new_keys, new_values, suffix_lengths, fork_list = args[5:]
    slots, width = suffix_keys.shape[1:]
    kv_local = width // HD
    rows = (kv_local + 2) * TILE
    assert queries.shape[0] == BRANCHES and fork_list.shape[0] == 1
    assert n * BRANCHES <= 256 and rows % 16 == 0 and n & (n - 1) == 0
    dma = pltpu.SemaphoreType.DMA
    hbm_spec = pl.BlockSpec(memory_space=pltpu.HBM)
    vmem_spec = pl.BlockSpec(memory_space=pltpu.VMEM)
    like = lambda x: pltpu.VMEM(x.shape, x.dtype)
    out_shape = (
        jax.ShapeDtypeStruct(queries.shape, BF16),
        jax.ShapeDtypeStruct(suffix_keys.shape, BF16),
        jax.ShapeDtypeStruct(suffix_values.shape, BF16),
    )
    results = pl.pallas_call(
        functools.partial(kernel, n),
        out_shape=out_shape,
        in_specs=[hbm_spec] * 9,
        out_specs=(vmem_spec,) * 3,
        scratch_shapes=[
            like(queries), like(prefix_keys), like(prefix_values), like(suffix_keys),
            like(suffix_values), like(new_keys), like(new_values),
            pltpu.SMEM(suffix_lengths.shape, jnp.int32), pltpu.SMEM(fork_list.shape, jnp.int32),
            pltpu.VMEM((rows, HD), F32),
            pltpu.VMEM((n, rows, HD), BF16),
            pltpu.VMEM((n, 2 * slots, width), BF16),
            pltpu.VMEM((n, rows, HD), BF16),
            pltpu.VMEM((n, rows, HD), BF16),
            pltpu.VMEM((rows, HD), F32),
            dma((9,)),
        ] + [dma((n,))] * 6,
        compiler_params=pltpu.CompilerParams(
            collective_id=0, has_side_effects=True, vmem_limit_bytes=32 * 2**20),
    )(*[pltpu.with_memory_space_constraint(x, pltpu.HBM) for x in args])
    return pl.pallas_call(
        place,
        out_shape=out_shape,
        in_specs=[vmem_spec] * 3,
        out_specs=(hbm_spec,) * 3,
        scratch_shapes=[dma((3,))],
        compiler_params=pltpu.CompilerParams(vmem_limit_bytes=2**20),
    )(*results)


def solution(mesh):
    return jax.shard_map(
        functools.partial(shards, mesh.shape["seq"]),
        mesh=mesh,
        in_specs=(
            P(("groups", "seq"), "mp"),
            P(("groups", "seq"), "mp"),
            P(("groups", "seq"), "mp"),
            P(("groups", "seq"), None, "mp"),
            P(("groups", "seq"), None, "mp"),
            P(("groups", "seq"), "mp"),
            P(("groups", "seq"), "mp"),
            P(("groups", "seq")),
            P(("groups", "seq"), None),
        ),
        out_specs=(
            P(("groups", "seq"), "mp"),
            P(("groups", "seq"), None, "mp"),
            P(("groups", "seq"), None, "mp"),
        ),
        check_vma=False,
    )
```
